256 devices in a mesh: clus: 16 (over y, x), fsdp: 8 (over z), head: 2 (over core).
Axes of the slice: x: 4, y: 4, z: 8, core: 2. Of those that a mesh axis runs over, the one named last changes fastest.
Arguments:
- feats: bfloat16 [32768, 2048], P(('clus', 'fsdp')), as said below
- w_query: float32 [2048, 2048], P(('clus', 'fsdp'), 'head'), may hold values from -0.125 to 0.125
- w_keyval: float32 [2048, 2048], P(('clus', 'fsdp'), 'head'), may hold values from -0.125 to 0.125
- grad_out: bfloat16 [32768, 2048], P(('clus', 'fsdp'), 'head'), may hold values from -6 to 6
- col_block: int32 [256, 5], replicated, may hold values from 0 to 255, as said below
- col_count: int32 [256], replicated, may hold values from 4 to 5
Outputs:
- out: bfloat16 [32768, 2048], P(('clus', 'fsdp'), 'head')
- grad_w_query: float32 [2048, 2048], P(('clus', 'fsdp'), 'head')
- grad_w_keyval: float32 [2048, 2048], P(('clus', 'fsdp'), 'head')
The draws below stay inside these ranges and needn't reach their ends.
Inputs may be any that keep to these rules, and one draw needn't show every extreme that they name: `col_block`: column 0 of row b is b itself; column 1 is another block of b's cluster (cluster of a block = block // 2); the other columns lie in other clusters whose index differs from b's cluster by a nonzero multiple of 8. A row names each block at most once. The rows of one cluster name, in any other cluster, at most one distinct block. `feats`: node features of order one, rows of differing scale.
All inputs are finite; a program needn't handle non-finite values.
Results may differ from the reference program's by a relative error of at most 0.014.
The reference program's roundings to bfloat16 on the way (of `wq`, `wkv`, `query`, `keyval`, `prob_b`, `dscore`, `dquery` and `dkeyval`) count: a program that leaves them out, or rounds other values in their place, can miss the bound.
Values may be sent and summed in bfloat16 or wider, within the bound.
A program may use at most 128 MiB of HBM per device.

```python
import math
import jax
import jax.numpy as jnp
from jax import lax

D = 2048
HEADS = 16
HD = 128
BLK = 128
NB_DEV = 2
NCOL = 5
CLUSTERS = 128
NBLK = 256
NODES = 32768
N_CLUS = 16
N_FSDP = 8


def draw_feats(key, part):
    first, second = jax.random.split(key, 2)
    base = jax.random.normal(first, (NODES, D), jnp.float32)
    scales = jnp.exp(jax.random.uniform(second, (NODES, 1), jnp.float32, 0.0, math.log(3.0)))
    return (base * scales).astype(jnp.bfloat16)


def draw_col_block(key, part):
    first, second, third = jax.random.split(key, 3)
    cluster_ids = jnp.arange(CLUSTERS, dtype=jnp.int32)
    clus_index = cluster_ids // N_FSDP
    fsdp_index = cluster_ids % N_FSDP
    local = jnp.arange(NB_DEV, dtype=jnp.int32)
    base = cluster_ids[:, None] * NB_DEV
    own = base + local[None, :]
    offset = jax.random.randint(first, (CLUSTERS, NB_DEV), 1, NB_DEV, dtype=jnp.int32)
    other = base + (local[None, :] + offset) % NB_DEV
    cluster_keys = jax.random.split(second, CLUSTERS)

    def peer_order(one_key):
        return jax.random.permutation(one_key, N_CLUS - 1).astype(jnp.int32)
    orders = jax.vmap(peer_order)(cluster_keys)
    source = jax.random.randint(third, (CLUSTERS, N_CLUS), 0, NB_DEV, dtype=jnp.int32)
    columns = [own, other]
    for column in range(NCOL - 2):
        position = (local * (NCOL - 2) + column) % (N_CLUS - 1)
        shifts = jnp.take(orders, position, axis=1)
        peers = (clus_index[:, None] + 1 + shifts) % N_CLUS
        chosen = jnp.take_along_axis(source, peers, axis=1)
        target = peers * N_FSDP + fsdp_index[:, None]
        columns.append(target * NB_DEV + chosen)
    return jnp.stack(columns, -1).reshape(NBLK, NCOL).astype(jnp.int32)


def place_ends(array, rng, low, top_value):
    extent = array.shape
    spot = [jax.random.randint(jax.random.fold_in(rng, axis), (), 0, extent[axis]) for axis in range(len(extent))]
    array = array.at[tuple(spot)].set(low)
    longest = extent.index(max(extent))
    spot[longest] = (spot[longest] + 1) % extent[longest]
    return array.at[tuple(spot)].set(top_value)


def shard_levels(stream_key, extent, pieces, least, top_value):
    factor_of = 1.0
    for dim, blocks in pieces:
        steps = jax.random.uniform(jax.random.fold_in(jax.random.fold_in(stream_key, 6), dim), (blocks,), jnp.float32, least / len(pieces), top_value / len(pieces))
        factor_of = factor_of * jnp.repeat(jnp.exp(steps), extent[dim] // blocks).reshape((-1,) + (1,) * (len(extent) - 1 - dim))
    return factor_of


def scatter_about(key, extent, width, reach, shards=(), kind=jnp.bfloat16):
    entries = width * jax.random.normal(key, extent, jnp.float32)
    if shards:
        entries = entries * shard_levels(key, extent, shards, -0.22, 0.18)
    return jnp.clip(entries, -reach, reach).astype(kind)


def setup_inputs(seed: int = 0) -> dict:
    seeds = jax.random.split(jax.random.key(seed), 7)
    feats = draw_feats(jax.random.fold_in(seeds[6], 71), 0)
    w_query = scatter_about(seeds[1], (D, D), D ** -0.5, 0.125, ((0, 128), (1, 2)), jnp.float32)
    w_keyval = scatter_about(seeds[2], (D, D), D ** -0.5, 0.125, ((0, 128), (1, 2)), jnp.float32)
    grad_out = scatter_about(seeds[3], (NODES, D), 1.0, 6.0, ((0, 128), (1, 2)))
    col_block = draw_col_block(jax.random.fold_in(seeds[6], 71), 0)
    col_count = place_ends(jax.random.randint(seeds[5], (NBLK,), NCOL - 1, NCOL + 1), jax.random.fold_in(seeds[5], 1), NCOL - 1, NCOL).astype(jnp.int32)
    return {"feats": feats, "w_query": w_query, "w_keyval": w_keyval, "grad_out": grad_out, "col_block": col_block, "col_count": col_count}


def reference(feats, w_query, w_keyval, grad_out, col_block, col_count):
    wq = w_query.astype(jnp.bfloat16)
    wkv = w_keyval.astype(jnp.bfloat16)
    query = jnp.dot(feats, wq, preferred_element_type=jnp.float32).astype(jnp.bfloat16)
    keyval = jnp.dot(feats, wkv, preferred_element_type=jnp.float32).astype(jnp.bfloat16)
    scale = 1.0 / math.sqrt(HD)
    panels = keyval.reshape(NBLK, BLK, HEADS, HD)
    queries = query.reshape(NBLK, BLK, HEADS, HD)
    cotans = grad_out.reshape(NBLK, BLK, HEADS, HD)

    def one_block(carry, index):
        cols = col_block[index]
        count = col_count[index]
        keys = panels[cols].reshape(NCOL * BLK, HEADS, HD).astype(jnp.float32)
        qblock = queries[index].astype(jnp.float32)
        gblock = cotans[index].astype(jnp.float32)
        valid = jnp.repeat(jnp.arange(NCOL, dtype=jnp.int32) < count, BLK)
        score = jnp.einsum('qhd,khd->hqk', qblock, keys) * scale
        score = jnp.where(valid[None, None, :], score, -1e+30)
        top = lax.optimization_barrier(jnp.max(score, axis=-1, keepdims=True))
        expo = jnp.exp(score - top)
        prob = expo / lax.optimization_barrier(jnp.sum(expo, axis=-1, keepdims=True))
        prob_b = prob.astype(jnp.bfloat16).astype(jnp.float32)
        out_block = jnp.einsum('hqk,khd->qhd', prob_b, keys).astype(jnp.bfloat16)
        dprob = jnp.einsum('qhd,khd->hqk', gblock, keys)
        delta = lax.optimization_barrier(jnp.sum(prob * dprob, axis=-1, keepdims=True))
        dscore = (prob * (dprob - delta)).astype(jnp.bfloat16).astype(jnp.float32)
        dquery = (jnp.einsum('hqk,khd->qhd', dscore, keys) * scale).astype(jnp.bfloat16)
        dkeys = jnp.einsum('hqk,qhd->khd', dscore, qblock) * scale + jnp.einsum('hqk,qhd->khd', prob_b, gblock)
        carry = carry.at[cols].add(dkeys.reshape(NCOL, BLK, HEADS, HD))
        return (carry, (out_block, dquery))
    start = jnp.zeros((NBLK, BLK, HEADS, HD), jnp.float32)
    totals, (out_blocks, dquery_blocks) = lax.scan(one_block, start, jnp.arange(NBLK, dtype=jnp.int32))
    out = out_blocks.reshape(NODES, D)
    dquery = dquery_blocks.reshape(NODES, D)
    dkeyval = totals.reshape(NODES, D).astype(jnp.bfloat16)
    rows_group = NB_DEV * BLK

    def add_group(carry, group):
        first = (group * rows_group).astype(jnp.int32)
        block_feats = lax.dynamic_slice_in_dim(feats, first, rows_group, 0)
        block_dq = lax.dynamic_slice_in_dim(dquery, first, rows_group, 0)
        block_dk = lax.dynamic_slice_in_dim(dkeyval, first, rows_group, 0)
        dims = (((0,), (0,)), ((), ()))
        term_q = lax.dot_general(block_feats, block_dq, dims, preferred_element_type=jnp.float32)
        term_k = lax.dot_general(block_feats, block_dk, dims, preferred_element_type=jnp.float32)
        term_q = lax.optimization_barrier(term_q.astype(jnp.bfloat16)).astype(jnp.float32)
        term_k = lax.optimization_barrier(term_k.astype(jnp.bfloat16)).astype(jnp.float32)
        return ((carry[0] + term_q, carry[1] + term_k), None)
    zeros = jnp.zeros((D, D), jnp.float32)
    (grad_q, grad_k), _ = lax.scan(add_group, (zeros, zeros), jnp.arange(CLUSTERS, dtype=jnp.int32))
    return (out, grad_q, grad_k)
```

```python
import functools
import math

import jax
import jax.numpy as jnp
from jax import lax
from jax.experimental import pallas as pl
from jax.experimental.pallas import tpu as pltpu
from jax.sharding import PartitionSpec as P

D = 2048
HD = 128
BLK = 128
NCOL = 5
SIDE = 4
NC = 16
NZ = 8
HALF = 1024
PER = 8
WROWS = 16
SCALE = 1.0 / math.sqrt(HD)
BF = jnp.bfloat16
F32 = jnp.float32
NT = (((1,), (1,)), ((), ()))
NN = (((1,), (0,)), ((), ()))


def here():
    return lax.axis_index("clus"), lax.axis_index("fsdp"), lax.axis_index("head")


def remote(src, dst, send, recv, device):
    return pltpu.make_async_remote_copy(
        src_ref=src,
        dst_ref=dst,
        send_sem=send,
        recv_sem=recv,
        device_id=device,
        device_id_type=pl.DeviceIdType.MESH,
    )


def greet_all(clus, fsdp, core):
    barrier = pltpu.get_barrier_semaphore()

    @pl.loop(0, 2 * NC)
    def _(i):
        other, side = i // 2, i % 2

        @pl.when(jnp.logical_or(other != clus, side != core))
        def _():
            pl.semaphore_signal(
                barrier, inc=1, device_id=(other, fsdp, side), device_id_type=pl.DeviceIdType.MESH
            )

    @pl.loop(1, NZ)
    def _(i):
        pl.semaphore_signal(
            barrier,
            inc=1,
            device_id=(clus, (fsdp + i) % NZ, core),
            device_id_type=pl.DeviceIdType.MESH,
        )

    pl.semaphore_wait(barrier, 2 * NC - 1 + NZ - 1)


def gather_kernel(
    feats,
    w_query,
    w_keyval,
    grad_out,
    feats_out,
    q_out,
    kv_out,
    cot_out,
    rows,
    wb,
    wall,
    ring_send,
    ring_recv,
    local_sem,
    save_sem,
    col_send,
    col_recv,
    z_send,
    z_recv,
    swap_send,
    swap_recv,
    cot_send,
    cot_recv,
    kv_send,
    kv_recv,
):
    clus, fsdp, core = here()
    xp, yp = clus % SIDE, clus // SIDE

    def at(dx, dy):
        return ((yp + dy) % SIDE) * SIDE + (xp + dx) % SIDE

    wb[0] = w_query[...].astype(BF)
    wb[1] = w_keyval[...].astype(BF)
    greet_all(clus, fsdp, core)

    def slot(half, first, second):
        return at(first, second) if half == 0 else at(second, first)

    def hop(half, axis, step):
        return slot(half, step, 0) if axis == 0 else slot(half, 0, step)

    def ring(half, label, src, part, own):
        index = half * 20 + label
        axis = 0 if label < 4 else 1
        step = 1 if label % 2 == 0 else -1
        start = half * 64 + (32 if part == 2 else 0)
        count = 64 if part == 0 else 32
        if own:
            source = feats.at[pl.ds(pl.multiple_of(core * BLK, BLK) + start, count)]
        else:
            source = rows.at[src, pl.ds(start, count)]
        return remote(
            source,
            rows.at[src, pl.ds(start, count)],
            ring_send.at[index],
            ring_recv.at[index],
            (hop(half, axis, step), fsdp, core),
        )

    OFF = (0, -1, 1, 2)
    plan = {}
    for half in (0, 1):
        plan[half, 0] = (slot(half, 0, 0), slot(half, -1, 0), 0)
        plan[half, 1] = (slot(half, 0, 0), slot(half, 1, 0), 0)
        plan[half, 2] = (slot(half, -1, 0), slot(half, -2, 0), 1)
        plan[half, 3] = (slot(half, 1, 0), slot(half, 2, 0), 2)
        for k, o in enumerate(OFF):
            base = 4 + 4 * k
            plan[half, base] = (slot(half, o, 0), slot(half, o, -1), 0)
            plan[half, base + 1] = (slot(half, o, 0), slot(half, o, 1), 0)
            plan[half, base + 2] = (slot(half, o, -1), slot(half, o, -2), 1)
            plan[half, base + 3] = (slot(half, o, 1), slot(half, o, 2), 2)

    def send(*labels):
        for label in labels:
            for half in (0, 1):
                src, _, part = plan[half, label]
                ring(half, label, src, part, label in (0, 1, 4, 5)).start()

    def arrived(*labels):
        for label in labels:
            for half in (0, 1):
                _, dst, part = plan[half, label]
                ring(half, label, dst, part, False).wait_recv()

    send(0, 1)

    def column_copy(j, part):
        head = core * PER + j
        src = wb.at[part, :, pl.ds(pl.multiple_of(j * HD, HD), HD)]
        dst = wall.at[part, clus, fsdp]
        return head, src, dst

    @pl.loop(0, PER)
    def _(i):
        j = (i + clus) % PER
        for part in (0, 1):
            head, src, dst = column_copy(j, part)
            mine = jnp.logical_and(head == clus, core == part)

            @pl.when(mine)
            def _():
                pltpu.make_async_copy(src, dst, col_recv.at[clus]).start()

            @pl.when(jnp.logical_not(mine))
            def _():
                remote(
                    src, dst, col_send.at[2 * j + part], col_recv.at[clus], (head, fsdp, part)
                ).start()

    own_rows = pltpu.make_async_copy(
        feats.at[pl.ds(pl.multiple_of(core * BLK, BLK), BLK)], rows.at[clus], local_sem
    )
    own_rows.start()
    send(4, 5)

    @pl.loop(0, NC)
    def _(i):
        remote(
            wb.at[0, :, pl.ds(0, HD)],
            wall.at[core, i, fsdp],
            col_send.at[0],
            col_recv.at[i],
            (clus, fsdp, 1 - core),
        ).wait_recv()

    def z_copy(i):
        other = (fsdp + i) % NZ
        return remote(
            wall.at[core, :, fsdp],
            wall.at[core, :, fsdp],
            z_send.at[i],
            z_recv.at[i],
            (clus, other, core),
        )

    @pl.loop(1, NZ)
    def _(i):
        z_copy(i).start()

    def cot_copy(j, block):
        head = core * PER + j
        src = grad_out.at[
            pl.ds(block * BLK, BLK), pl.ds(pl.multiple_of(j * HD, HD), HD)
        ]
        return head, src, cot_out.at[clus]

    @pl.loop(0, PER)
    def _(i):
        j = (i + clus) % PER
        for block in (0, 1):
            head, src, dst = cot_copy(j, block)
            mine = jnp.logical_and(head == clus, core == block)

            @pl.when(mine)
            def _():
                pltpu.make_async_copy(src, dst, cot_recv.at[clus]).start()

            @pl.when(jnp.logical_not(mine))
            def _():
                remote(
                    src, dst, cot_send.at[2 * j + block], cot_recv.at[clus], (head, fsdp, block)
                ).start()

    arrived(0, 1)
    send(2, 3, 8, 9, 12, 13)

    @pl.loop(1, NZ)
    def _(i):
        other = (fsdp + NZ - i) % NZ
        remote(
            wall.at[core, :, other],
            wall.at[core, :, other],
            z_send.at[i],
            z_recv.at[i],
            (clus, other, core),
        ).wait_recv()

    swap = remote(
        wall.at[core], wall.at[core], swap_send, swap_recv, (clus, fsdp, 1 - core)
    )
    swap.start()
    arrived(4, 5)
    send(6, 7)
    arrived(2, 3)
    send(16, 17)
    remote(
        wall.at[1 - core], wall.at[1 - core], swap_send, swap_recv, (clus, fsdp, 1 - core)
    ).wait_recv()
    own_rows.wait()

    saved = []
    shared = []

    def project(dx, dy):
        src = at(dx, dy)
        index = len(saved)
        save = pltpu.make_async_copy(rows.at[src], feats_out.at[src], save_sem.at[index])
        save.start()
        weights = jnp.concatenate(
            [wall[0].reshape(D, HD), wall[1].reshape(D, HD)], axis=1
        )
        both = lax.dot_general(rows[src], weights, NN, preferred_element_type=F32)
        q_out[src] = both[:, :HD].astype(BF)
        keys = both[:, HD:]
        mine = 2 * src + core
        kv_out[mine, 0] = keys.astype(BF)
        kv_out[mine, 1] = keys.T.astype(BF)
        share = remote(
            kv_out.at[mine],
            kv_out.at[mine],
            kv_send.at[index],
            kv_recv.at[index],
            (clus, fsdp, 1 - core),
        )
        share.start()
        theirs = 2 * src + 1 - core
        saved.append(save)
        shared.append(
            (
                share,
                remote(
                    kv_out.at[theirs],
                    kv_out.at[theirs],
                    kv_send.at[index],
                    kv_recv.at[index],
                    (clus, fsdp, 1 - core),
                ),
            )
        )

    project(0, 0)
    arrived(8, 9, 12, 13)
    send(10, 11, 14, 15)
    project(1, 0)
    project(-1, 0)
    project(0, 1)
    arrived(16, 17)
    send(18, 19)
    project(0, -1)
    project(1, 1)
    project(-1, 1)
    project(1, -1)
    project(-1, -1)
    arrived(6, 7)
    project(2, 0)
    project(0, 2)
    arrived(10, 11, 14, 15)
    project(2, 1)
    project(2, -1)
    project(1, 2)
    project(-1, 2)
    arrived(18, 19)
    project(2, 2)

    @pl.loop(0, NC)
    def _(i):
        remote(
            grad_out.at[pl.ds(0, BLK), pl.ds(0, HD)],
            cot_out.at[i],
            cot_send.at[0],
            cot_recv.at[i],
            (clus, fsdp, 1 - core),
        ).wait_recv()

    @pl.loop(0, PER)
    def _(j):
        for part in (0, 1):
            head, src, dst = column_copy(j, part)
            _, csrc, cdst = cot_copy(j, part)

            @pl.when(jnp.logical_not(jnp.logical_and(head == clus, core == part)))
            def _():
                remote(
                    src, dst, col_send.at[2 * j + part], col_recv.at[clus], (head, fsdp, part)
                ).wait_send()
                remote(
                    csrc, cdst, cot_send.at[2 * j + part], cot_recv.at[clus], (head, fsdp, part)
                ).wait_send()

    @pl.loop(1, NZ)
    def _(i):
        z_copy(i).wait_send()

    swap.wait_send()
    for label in range(20):
        for half in (0, 1):
            src, _, part = plan[half, label]
            ring(half, label, src, part, label in (0, 1, 4, 5)).wait_send()
    for save, (share, theirs) in zip(saved, shared):
        save.wait()
        share.wait_send()
        theirs.wait_recv()


def attend_kernel(q, kv, cot, col_block, col_count, out, dqt, own, sib, total):
    clus, fsdp, core = here()
    total[...] = jnp.zeros_like(total)

    def step(i, carry):
        block = 2 * NZ * i + 2 * fsdp + core
        cols = [col_block[block, k] for k in range(NCOL)]
        cols = [(c // (2 * NZ)) * 2 + c % 2 for c in cols]
        count = col_count[block]
        query, grad = q[i], cot[i]
        keys = jnp.concatenate([kv[c, 0] for c in cols], axis=0)
        keys_t = jnp.concatenate([kv[c, 1] for c in cols], axis=1)
        both = lax.dot_general(
            keys, jnp.concatenate([query, grad], axis=0), NT, preferred_element_type=F32
        )
        score = both[:, :BLK] * SCALE
        dprob = both[:, BLK:]
        place = lax.broadcasted_iota(jnp.int32, score.shape, 0) // BLK
        score = jnp.where(place < count, score, -1e30)
        top = jnp.max(score, axis=0, keepdims=True)
        expo = jnp.exp(score - top)
        prob = expo * (1.0 / jnp.sum(expo, axis=0, keepdims=True))
        delta = jnp.sum(prob * dprob, axis=0, keepdims=True)
        dscore = (prob * (dprob - delta)).astype(BF)
        prob_b = prob.astype(BF)
        both_t = lax.dot_general(
            keys_t,
            jnp.concatenate([dscore, prob_b], axis=1),
            NN,
            preferred_element_type=F32,
        )
        dqt[:, pl.ds(pl.multiple_of(i * BLK, BLK), BLK)] = (both_t[:, :BLK] * SCALE).astype(BF)
        out[i] = both_t[:, BLK:].T.astype(BF)
        dkeys = (
            lax.dot_general(dscore, query, NN, preferred_element_type=F32) * SCALE
            + lax.dot_general(prob_b, grad, NN, preferred_element_type=F32)
        )
        for k, c in enumerate(cols):
            total[c // 2, c % 2] += dkeys[k * BLK : (k + 1) * BLK]
        return carry

    lax.fori_loop(0, NC, step, 0, unroll=2)
    own[...] = total[:, core]
    sib[...] = total[:, 1 - core].astype(BF)


def scatter_kernel(
    feats,
    out_blocks,
    dqt,
    own,
    sib,
    out,
    grad_q,
    grad_k,
    rows,
    other,
    dkt,
    part_send,
    part_recv,
    part_own,
    z_out,
    z_in,
    fin,
    load_sem,
    dk_sem,
    out_send,
    out_recv,
    half_send,
    half_recv,
    z_send,
    z_recv,
    fin_send,
    fin_recv,
):
    clus, fsdp, core = here()
    CH = 256
    NCH = D // CH
    greet_all(clus, fsdp, core)
    give = remote(sib, other, dk_sem.at[0], dk_sem.at[1], (clus, fsdp, 1 - core))
    give.start()

    def chunk(n):
        return (n + (1 - core) * (NCH // 2)) % NCH

    def load(n):
        cols = pl.ds(pl.multiple_of(chunk(n) * CH, CH), CH)
        return pltpu.make_async_copy(
            feats.at[:, :, cols], rows.at[:, :, cols], load_sem.at[n]
        )

    for n in range(NCH):
        load(n).start()

    def out_copy(s):
        return remote(
            out_blocks.at[s],
            out.at[
                pl.ds(pl.multiple_of(core * BLK, BLK), BLK),
                pl.ds(pl.multiple_of((clus % PER) * HD, HD), HD),
            ],
            out_send.at[s],
            out_recv.at[2 * (clus % PER) + core],
            (s, fsdp, clus // PER),
        )

    own_out = core == clus // PER

    @pl.loop(0, NC)
    def _(i):
        s = (i + clus) % NC
        mine = jnp.logical_and(s == clus, own_out)

        @pl.when(mine)
        def _():
            pltpu.make_async_copy(
                out_blocks.at[s],
                out.at[
                    pl.ds(pl.multiple_of(core * BLK, BLK), BLK),
                    pl.ds(pl.multiple_of((clus % PER) * HD, HD), HD),
                ],
                out_recv.at[2 * (clus % PER) + core],
            ).start()

        @pl.when(jnp.logical_not(mine))
        def _():
            out_copy(s).start()

    def half_copy(t):
        return remote(
            part_send.at[t],
            part_recv.at[t],
            half_send.at[t],
            half_recv.at[t],
            (clus, fsdp, 1 - core),
        )

    def z_copy(t, i):
        to = (fsdp + i) % NZ
        return remote(
            z_out.at[t, to],
            z_in.at[t, fsdp],
            z_send.at[t, i],
            z_recv.at[t, i],
            (clus, to, core),
        )

    def gradient(t, lhs):
        for n in range(NCH):
            if t == 0:
                load(n).wait()
            cols = pl.ds(pl.multiple_of(chunk(n) * CH, CH), CH)
            part = lax.dot_general(
                lhs[...],
                rows[:, :, cols].reshape(NC * BLK, CH),
                NN,
                preferred_element_type=F32,
            )
            for k in range(CH // BLK):
                piece = part[:, k * BLK : (k + 1) * BLK].T.reshape(NZ, WROWS, HD)
                index = (n * CH) // BLK + k
                if index < PER:
                    part_send[t, index] = piece.astype(BF)
                else:
                    part_own[t, index - PER] = piece
            if n == NCH // 2 - 1:
                half_copy(t).start()
        half_copy(t).wait_recv()
        for k in range(PER):
            total = part_own[t, k] + part_recv[t, k].astype(F32)
            part_own[t, k] = total
            z_out[t, :, k] = total.astype(BF)

        @pl.loop(1, NZ)
        def _(i):
            z_copy(t, i).start()

    gradient(0, dqt)
    give.wait_recv()
    for s in range(NC):
        total = own[s] + other[s].astype(F32)
        dkt[:, s * BLK : (s + 1) * BLK] = total.astype(BF).astype(F32).T.astype(BF)
    gradient(1, dkt)

    def fin_copy(t, k):
        dest = (grad_q, grad_k)[t]
        to = core * PER + k
        return (
            to,
            fin.at[t, k],
            dest.at[:, pl.ds(pl.multiple_of((clus % PER) * HD, HD), HD)],
            fin_recv.at[t, clus % PER],
        )

    for t in (0, 1):
        for i in range(1, NZ):
            frm = (fsdp + NZ - i) % NZ
            remote(
                z_out.at[t, 0],
                z_in.at[t, frm],
                z_send.at[t, i],
                z_recv.at[t, i],
                (clus, frm, core),
            ).wait_recv()
        for k in range(PER):
            total = part_own[t, k, fsdp]
            for i in range(1, NZ):
                total += z_in[t, (fsdp + NZ - i) % NZ, k].astype(F32)
            fin[t, k] = total
        for k in range(PER):
            to, src, dst, recv = fin_copy(t, k)

            @pl.when(to == clus)
            def _():
                pltpu.make_async_copy(src, dst, recv).start()

            @pl.when(to != clus)
            def _():
                remote(src, dst, fin_send.at[t, k], recv, (to, fsdp, clus // PER)).start()

    give.wait_send()
    for t in (0, 1):
        half_copy(t).wait_send()

        @pl.loop(1, NZ)
        def _(i):
            z_copy(t, i).wait_send()

        for k in range(PER):
            to, src, dst, recv = fin_copy(t, k)

            @pl.when(to != clus)
            def _():
                remote(src, dst, fin_send.at[t, k], recv, (to, fsdp, clus // PER)).wait_send()

    @pl.loop(0, NC)
    def _(s):
        @pl.when(jnp.logical_not(jnp.logical_and(s == clus, own_out)))
        def _():
            out_copy(s).wait_send()

    for m in range(PER):
        for block in (0, 1):
            remote(
                out_blocks.at[0],
                out.at[pl.ds(block * BLK, BLK), pl.ds(m * HD, HD)],
                out_send.at[0],
                out_recv.at[2 * m + block],
                (clus, fsdp, 1 - core),
            ).wait_recv()
        for t in (0, 1):
            remote(
                fin.at[t, 0],
                (grad_q, grad_k)[t].at[:, pl.ds(m * HD, HD)],
                fin_send.at[t, 0],
                fin_recv.at[t, m],
                (clus, fsdp, 1 - core),
            ).wait_recv()


ANY = pl.BlockSpec(memory_space=pl.ANY)
VM = pl.BlockSpec(memory_space=pltpu.VMEM)
SM = pl.BlockSpec(memory_space=pltpu.SMEM)
DMA = pltpu.SemaphoreType.DMA
LIMIT = 56 * 1024 * 1024


def shape(dims, kind):
    return jax.ShapeDtypeStruct(dims, kind)


def on_device(feats, w_query, w_keyval, grad_out, col_block, col_count):
    feats_all, query, keyval, cots = pl.pallas_call(
        gather_kernel,
        name="gather_project",
        out_shape=(
            shape((NC, BLK, D), BF),
            shape((NC, BLK, HD), BF),
            shape((2 * NC, 2, BLK, HD), BF),
            shape((NC, BLK, HD), BF),
        ),
        in_specs=[ANY, VM, VM, ANY],
        out_specs=(ANY, VM, VM, VM),
        scratch_shapes=[
            pltpu.VMEM((NC, BLK, D), BF),
            pltpu.VMEM((2, WROWS, HALF), BF),
            pltpu.VMEM((2, NC, NZ, WROWS, HD), BF),
            DMA((40,)),
            DMA((40,)),
            DMA,
            DMA((NC,)),
            DMA((16,)),
            DMA((NC,)),
            DMA((NZ,)),
            DMA((NZ,)),
            DMA,
            DMA,
            DMA((16,)),
            DMA((NC,)),
            DMA((NC,)),
            DMA((NC,)),
        ],
        compiler_params=pltpu.CompilerParams(
            collective_id=1, has_side_effects=True, vmem_limit_bytes=LIMIT
        ),
        cost_estimate=pl.CostEstimate(
            flops=2 * D * D * 256, bytes_accessed=18 << 20, transcendentals=0
        ),
    )(feats, w_query, w_keyval, grad_out)
    out_blocks, dqt, own, sib = pl.pallas_call(
        attend_kernel,
        name="attend",
        out_shape=(
            shape((NC, BLK, HD), BF),
            shape((HD, NC * BLK), BF),
            shape((NC, BLK, HD), F32),
            shape((NC, BLK, HD), BF),
        ),
        in_specs=[VM, VM, VM, SM, SM],
        out_specs=(VM, VM, VM, VM),
        scratch_shapes=[pltpu.VMEM((NC, 2, BLK, HD), F32)],
        compiler_params=pltpu.CompilerParams(vmem_limit_bytes=LIMIT),
        cost_estimate=pl.CostEstimate(
            flops=12 * NC * BLK * 640 * HD, bytes_accessed=6 << 20, transcendentals=NC * BLK * 640
        ),
    )(query, keyval, cots, col_block, col_count)
    return pl.pallas_call(
        scatter_kernel,
        name="scatter_grads",
        out_shape=(
            shape((2 * BLK, HALF), BF),
            shape((WROWS, HALF), F32),
            shape((WROWS, HALF), F32),
        ),
        in_specs=[ANY, VM, VM, VM, VM],
        out_specs=(VM, VM, VM),
        scratch_shapes=[
            pltpu.VMEM((NC, BLK, D), BF),
            pltpu.VMEM((NC, BLK, HD), BF),
            pltpu.VMEM((HD, NC * BLK), BF),
            pltpu.VMEM((2, PER, NZ, WROWS, HD), BF),
            pltpu.VMEM((2, PER, NZ, WROWS, HD), BF),
            pltpu.VMEM((2, PER, NZ, WROWS, HD), F32),
            pltpu.VMEM((2, NZ, PER, WROWS, HD), BF),
            pltpu.VMEM((2, NZ, PER, WROWS, HD), BF),
            pltpu.VMEM((2, PER, WROWS, HD), F32),
            DMA((8,)),
            DMA((2,)),
            DMA((NC,)),
            DMA((NC,)),
            DMA((2,)),
            DMA((2,)),
            DMA((2, NZ)),
            DMA((2, NZ)),
            DMA((2, PER)),
            DMA((2, PER)),
        ],
        compiler_params=pltpu.CompilerParams(
            collective_id=2, has_side_effects=True, vmem_limit_bytes=LIMIT
        ),
        cost_estimate=pl.CostEstimate(
            flops=2 * D * D * 256, bytes_accessed=12 << 20, transcendentals=0
        ),
    )(feats_all, out_blocks, dqt, own, sib)


def solution(mesh):
    return jax.shard_map(
        on_device,
        mesh=mesh,
        in_specs=(
            P(("clus", "fsdp"), None),
            P(("clus", "fsdp"), "head"),
            P(("clus", "fsdp"), "head"),
            P(("clus", "fsdp"), "head"),
            P(),
            P(),
        ),
        out_specs=(
            P(("clus", "fsdp"), "head"),
            P(("clus", "fsdp"), "head"),
            P(("clus", "fsdp"), "head"),
        ),
        check_vma=False,
    )
```

```python
import functools
import math

import jax
import jax.numpy as jnp
from jax import lax
from jax.experimental import pallas as pl
from jax.experimental.pallas import tpu as pltpu
from jax.sharding import PartitionSpec as P

D = 2048
HD = 128
BLK = 128
NCOL = 5
SIDE = 4
NC = 16
NZ = 8
HALF = 1024
PER = 8
WROWS = 16
SCALE = 1.0 / math.sqrt(HD)
LOG2 = SCALE / math.log(2.0)
BF = jnp.bfloat16
F32 = jnp.float32
NT = (((1,), (1,)), ((), ()))
NN = (((1,), (0,)), ((), ()))


def here():
    return lax.axis_index("clus"), lax.axis_index("fsdp"), lax.axis_index("head")


def remote(src, dst, send, recv, device):
    return pltpu.make_async_remote_copy(
        src_ref=src,
        dst_ref=dst,
        send_sem=send,
        recv_sem=recv,
        device_id=device,
        device_id_type=pl.DeviceIdType.MESH,
    )


def greet(clus, fsdp, core):
    barrier = pltpu.get_barrier_semaphore()

    @pl.loop(0, NC)
    def _(i):
        for side in (0, 1):

            @pl.when(jnp.logical_or(i != clus, side != core))
            def _():
                pl.semaphore_signal(
                    barrier, inc=1, device_id=(i, fsdp, side), device_id_type=pl.DeviceIdType.MESH
                )

    @pl.loop(1, NZ)
    def _(i):
        pl.semaphore_signal(
            barrier,
            inc=1,
            device_id=(clus, (fsdp + i) % NZ, core),
            device_id_type=pl.DeviceIdType.MESH,
        )


def greeted():
    pl.semaphore_wait(pltpu.get_barrier_semaphore(), 2 * NC - 1 + NZ - 1)


def gather_kernel(
    feats,
    w_query,
    w_keyval,
    grad_out,
    rows,
    q_out,
    kv_out,
    cot_out,
    wb,
    wall,
    ring_send,
    ring_recv,
    local_sem,
    col_send,
    col_recv,
    z_send,
    z_recv,
    swap_send,
    swap_recv,
    cot_send,
    cot_recv,
    kv_send,
    kv_recv,
):
    clus, fsdp, core = here()
    xp, yp = clus % SIDE, clus // SIDE

    def at(dx, dy):
        return ((yp + dy) % SIDE) * SIDE + (xp + dx) % SIDE

    greet(clus, fsdp, core)
    wb[0] = w_query[...].astype(BF)
    wb[1] = w_keyval[...].astype(BF)
    greeted()

    def slot(half, first, second):
        return at(first, second) if half == 0 else at(second, first)

    def hop(half, axis, step):
        return slot(half, step, 0) if axis == 0 else slot(half, 0, step)

    def ring(half, label, src, part, own):
        index = half * 20 + label
        axis = 0 if label < 4 else 1
        step = 1 if label % 2 == 0 else -1
        start = half * 64 + (32 if part == 2 else 0)
        count = 64 if part == 0 else 32
        if own:
            source = feats.at[pl.ds(pl.multiple_of(core * BLK, BLK) + start, count)]
        else:
            source = rows.at[src, pl.ds(start, count)]
        return remote(
            source,
            rows.at[src, pl.ds(start, count)],
            ring_send.at[index],
            ring_recv.at[index],
            (hop(half, axis, step), fsdp, core),
        )

    OFF = (0, -1, 1, 2)
    plan = {}
    for half in (0, 1):
        plan[half, 0] = (slot(half, 0, 0), slot(half, -1, 0), 0)
        plan[half, 1] = (slot(half, 0, 0), slot(half, 1, 0), 0)
        plan[half, 2] = (slot(half, -1, 0), slot(half, -2, 0), 1)
        plan[half, 3] = (slot(half, 1, 0), slot(half, 2, 0), 2)
        for k, o in enumerate(OFF):
            base = 4 + 4 * k
            plan[half, base] = (slot(half, o, 0), slot(half, o, -1), 0)
            plan[half, base + 1] = (slot(half, o, 0), slot(half, o, 1), 0)
            plan[half, base + 2] = (slot(half, o, -1), slot(half, o, -2), 1)
            plan[half, base + 3] = (slot(half, o, 1), slot(half, o, 2), 2)

    def send(*labels):
        for label in labels:
            for half in (0, 1):
                src, _, part = plan[half, label]
                ring(half, label, src, part, label in (0, 1, 4, 5)).start()

    def arrived(*labels):
        for label in labels:
            for half in (0, 1):
                _, dst, part = plan[half, label]
                ring(half, label, dst, part, False).wait_recv()

    send(0, 1)

    def column_copy(j, part):
        head = core * PER + j
        src = wb.at[part, :, pl.ds(pl.multiple_of(j * HD, HD), HD)]
        dst = wall.at[part, clus, fsdp]
        return head, src, dst

    @pl.loop(0, PER)
    def _(i):
        j = (i + clus) % PER
        for part in (0, 1):
            head, src, dst = column_copy(j, part)
            mine = jnp.logical_and(head == clus, core == part)

            @pl.when(mine)
            def _():
                pltpu.make_async_copy(src, dst, col_recv.at[clus]).start()

            @pl.when(jnp.logical_not(mine))
            def _():
                remote(
                    src, dst, col_send.at[2 * j + part], col_recv.at[clus], (head, fsdp, part)
                ).start()

    own_rows = pltpu.make_async_copy(
        feats.at[pl.ds(pl.multiple_of(core * BLK, BLK), BLK)], rows.at[clus], local_sem
    )
    own_rows.start()
    send(4, 5)

    @pl.loop(0, NC)
    def _(i):
        remote(
            wb.at[0, :, pl.ds(0, HD)],
            wall.at[core, i, fsdp],
            col_send.at[0],
            col_recv.at[i],
            (clus, fsdp, 1 - core),
        ).wait_recv()

    def z_copy(i):
        other = (fsdp + i) % NZ
        return remote(
            wall.at[core, :, fsdp],
            wall.at[core, :, fsdp],
            z_send.at[i],
            z_recv.at[i],
            (clus, other, core),
        )

    @pl.loop(1, NZ)
    def _(i):
        z_copy(i).start()

    def cot_copy(j, block):
        head = core * PER + j
        src = grad_out.at[
            pl.ds(block * BLK, BLK), pl.ds(pl.multiple_of(j * HD, HD), HD)
        ]
        return head, src, cot_out.at[clus]

    @pl.loop(0, PER)
    def _(i):
        j = (i + clus) % PER
        for block in (0, 1):
            head, src, dst = cot_copy(j, block)
            mine = jnp.logical_and(head == clus, core == block)

            @pl.when(mine)
            def _():
                pltpu.make_async_copy(src, dst, cot_recv.at[clus]).start()

            @pl.when(jnp.logical_not(mine))
            def _():
                remote(
                    src, dst, cot_send.at[2 * j + block], cot_recv.at[clus], (head, fsdp, block)
                ).start()

    arrived(0, 1)
    send(2, 3, 8, 9, 12, 13)

    @pl.loop(1, NZ)
    def _(i):
        other = (fsdp + NZ - i) % NZ
        remote(
            wall.at[core, :, other],
            wall.at[core, :, other],
            z_send.at[i],
            z_recv.at[i],
            (clus, other, core),
        ).wait_recv()

    swap = remote(
        wall.at[core], wall.at[core], swap_send, swap_recv, (clus, fsdp, 1 - core)
    )
    swap.start()
    arrived(4, 5)
    send(6, 7)
    arrived(2, 3)
    send(16, 17)
    remote(
        wall.at[1 - core], wall.at[1 - core], swap_send, swap_recv, (clus, fsdp, 1 - core)
    ).wait_recv()
    own_rows.wait()

    shared = []

    def project(dx, dy):
        src = at(dx, dy)
        index = len(shared)
        weights = jnp.concatenate(
            [wall[0].reshape(D, HD), wall[1].reshape(D, HD)], axis=1
        )
        both = lax.dot_general(rows[src], weights, NN, preferred_element_type=F32)
        q_out[src] = both[:, :HD].astype(BF)
        keys = both[:, HD:]
        mine = 2 * src + core
        kv_out[mine, 0] = keys.astype(BF)
        kv_out[mine, 1] = keys.T.astype(BF)
        share = remote(
            kv_out.at[mine],
            kv_out.at[mine],
            kv_send.at[index],
            kv_recv.at[index],
            (clus, fsdp, 1 - core),
        )
        share.start()
        theirs = 2 * src + 1 - core
        shared.append(
            (
                share,
                remote(
                    kv_out.at[theirs],
                    kv_out.at[theirs],
                    kv_send.at[index],
                    kv_recv.at[index],
                    (clus, fsdp, 1 - core),
                ),
            )
        )

    project(0, 0)
    arrived(8, 9, 12, 13)
    send(10, 11, 14, 15)
    project(1, 0)
    project(-1, 0)
    project(0, 1)
    arrived(16, 17)
    send(18, 19)
    project(0, -1)
    project(1, 1)
    project(-1, 1)
    project(1, -1)
    project(-1, -1)
    arrived(6, 7)
    project(2, 0)
    project(0, 2)
    arrived(10, 11, 14, 15)
    project(2, 1)
    project(2, -1)
    project(1, 2)
    project(-1, 2)
    arrived(18, 19)
    project(2, 2)

    @pl.loop(0, NC)
    def _(i):
        remote(
            grad_out.at[pl.ds(0, BLK), pl.ds(0, HD)],
            cot_out.at[i],
            cot_send.at[0],
            cot_recv.at[i],
            (clus, fsdp, 1 - core),
        ).wait_recv()

    @pl.loop(0, PER)
    def _(j):
        for part in (0, 1):
            head, src, dst = column_copy(j, part)
            _, csrc, cdst = cot_copy(j, part)

            @pl.when(jnp.logical_not(jnp.logical_and(head == clus, core == part)))
            def _():
                remote(
                    src, dst, col_send.at[2 * j + part], col_recv.at[clus], (head, fsdp, part)
                ).wait_send()
                remote(
                    csrc, cdst, cot_send.at[2 * j + part], cot_recv.at[clus], (head, fsdp, part)
                ).wait_send()

    @pl.loop(1, NZ)
    def _(i):
        z_copy(i).wait_send()

    swap.wait_send()
    for label in range(20):
        for half in (0, 1):
            src, _, part = plan[half, label]
            ring(half, label, src, part, label in (0, 1, 4, 5)).wait_send()
    for share, theirs in shared:
        share.wait_send()
        theirs.wait_recv()


def attend_kernel(q, kv, cot, col_block, col_count, out, dqt, total):
    clus, fsdp, core = here()
    total[...] = jnp.zeros_like(total)

    def stage_one(i):
        block = 2 * NZ * i + 2 * fsdp + core
        cols = [col_block[k, block] for k in range(NCOL)]
        cols = [(c // (2 * NZ)) * 2 + c % 2 for c in cols]
        live = col_count[block] == NCOL
        query, grad = q[i], cot[i]
        pair = jnp.concatenate([query, grad], axis=0)
        both = [
            lax.dot_general(kv[c, 0], pair, NT, preferred_element_type=F32) for c in cols
        ]
        return cols, live, query, grad, both

    def stage_two(cols, live, query, grad, both):
        scores = [x[:, :BLK] for x in both]
        scores[-1] = jnp.where(live, scores[-1], -1e30)
        top = functools.reduce(jnp.maximum, scores)
        top = jnp.max(top, axis=0, keepdims=True)
        expos = [jnp.exp2((x - top) * LOG2) for x in scores]
        norm = jnp.sum(functools.reduce(jnp.add, expos), axis=0, keepdims=True)
        inv = 1.0 / norm
        probs = [x * inv for x in expos]
        delta = functools.reduce(jnp.add, [p * x[:, BLK:] for p, x in zip(probs, both)])
        delta = jnp.sum(delta, axis=0, keepdims=True)
        ds = [(p * SCALE * (x[:, BLK:] - delta)).astype(BF) for p, x in zip(probs, both)]
        return ds, [p.astype(BF) for p in probs]

    def stage_three(i, cols, query, grad, ds, pb):
        keys_t = jnp.concatenate([kv[c, 1] for c in cols], axis=1)
        right = jnp.concatenate(
            [jnp.concatenate(ds, axis=0), jnp.concatenate(pb, axis=0)], axis=1
        )
        both_t = lax.dot_general(keys_t, right, NN, preferred_element_type=F32)
        dqt[:, pl.ds(pl.multiple_of(i * BLK, BLK), BLK)] = both_t[:, :BLK].astype(BF)
        out[i] = both_t[:, BLK:].T.astype(BF)
        pair = jnp.concatenate([query, grad], axis=0)
        for k, c in enumerate(cols):
            total[c // 2, c % 2] += lax.dot_general(
                jnp.concatenate([ds[k], pb[k]], axis=1), pair, NN, preferred_element_type=F32
            )

    GROUP = 4

    def step(n, carry):
        items = [n * GROUP + g for g in range(GROUP)]
        ones = [stage_one(i) for i in items]
        twos = [stage_two(*o) for o in ones]
        for i, o, t in zip(items, ones, twos):
            stage_three(i, o[0], o[2], o[3], *t)
        return carry

    lax.fori_loop(0, NC // GROUP, step, 0)


def scatter_kernel(
    feats,
    out_blocks,
    dqt,
    dkv,
    out,
    grad_q,
    grad_k,
    other,
    dkt,
    part_send,
    part_recv,
    part_own,
    z_out,
    z_in,
    fin,
    dk_sem,
    out_send,
    out_recv,
    half_send,
    half_recv,
    z_send,
    z_recv,
    fin_send,
    fin_recv,
):
    clus, fsdp, core = here()
    greet(clus, fsdp, core)
    sibling = (clus, fsdp, 1 - core)
    give = remote(dkv.at[:, 1 - core], other, dk_sem.at[0], dk_sem.at[1], sibling)

    def out_spot():
        return out.at[
            pl.ds(pl.multiple_of(core * BLK, BLK), BLK),
            pl.ds(pl.multiple_of((clus % PER) * HD, HD), HD),
        ]

    def out_copy(s):
        return remote(
            out_blocks.at[s],
            out_spot(),
            out_send.at[s],
            out_recv.at[2 * (clus % PER) + core],
            (s, fsdp, clus // PER),
        )

    own_out = core == clus // PER

    def send_out():
        @pl.loop(0, NC)
        def _(i):
            s = (i + clus) % NC
            mine = jnp.logical_and(s == clus, own_out)

            @pl.when(mine)
            def _():
                pltpu.make_async_copy(
                    out_blocks.at[s], out_spot(), out_recv.at[2 * (clus % PER) + core]
                ).start()

            @pl.when(jnp.logical_not(mine))
            def _():
                out_copy(s).start()

    def half_copy(t):
        return remote(
            part_send.at[t], part_recv.at[t], half_send.at[t], half_recv.at[t], sibling
        )

    def z_copy(t, g, i):
        to = (fsdp + i) % NZ
        return remote(
            z_out.at[t, g, to],
            z_in.at[t, g, fsdp],
            z_send.at[2 * t + g, i],
            z_recv.at[2 * t + g, i],
            (clus, to, core),
        )

    CH = 2 * BLK

    def chunk(lhs, n, side):
        cols = pl.ds(pl.multiple_of(side * HALF + n * CH, CH), CH)
        part = lax.dot_general(
            lhs[...],
            feats[:, :, cols].reshape(NC * BLK, CH),
            NN,
            preferred_element_type=F32,
        )
        return [part[:, k * BLK : (k + 1) * BLK].T.reshape(NZ, WROWS, HD) for k in (0, 1)]

    def for_sibling(t, lhs):
        for n in range(PER // 2):
            for k, piece in enumerate(chunk(lhs, n, 1 - core)):
                part_send[t, 2 * n + k] = piece.astype(BF)

    def for_self(t, lhs):
        for n in range(PER // 2):
            for k, piece in enumerate(chunk(lhs, n, core)):
                part_own[t, 2 * n + k] = piece
            if n == 1:
                half_copy(t).wait_recv()
            if n % 2 == 1:
                g = n // 2
                for k in range(PER // 2):
                    at = g * (PER // 2) + k
                    total = part_own[t, at] + part_recv[t, at].astype(F32)
                    part_own[t, at] = total
                    z_out[t, g, :, k] = total.astype(BF)

                @pl.loop(1, NZ)
                def _(i):
                    z_copy(t, g, i).start()

    for_sibling(0, dqt)
    greeted()
    give.start()
    half_copy(0).start()
    for_self(0, dqt)
    give.wait_recv()
    for s in range(NC):
        total = (dkv[s, core] + other[s]).astype(BF).astype(F32)
        dkt[:, s * BLK : (s + 1) * BLK] = total.T.astype(BF)
    for_sibling(1, dkt)
    half_copy(1).start()
    for_self(1, dkt)
    send_out()

    def fin_copy(t, k):
        dest = (grad_q, grad_k)[t]
        to = core * PER + k
        return (
            to,
            fin.at[t, k],
            dest.at[:, pl.ds(pl.multiple_of((clus % PER) * HD, HD), HD)],
            fin_recv.at[t, clus % PER],
        )

    for t in (0, 1):
        for g in (0, 1):
            for i in range(1, NZ):
                frm = (fsdp + NZ - i) % NZ
                remote(
                    z_out.at[t, g, 0],
                    z_in.at[t, g, frm],
                    z_send.at[2 * t + g, i],
                    z_recv.at[2 * t + g, i],
                    (clus, frm, core),
                ).wait_recv()
            for k in range(PER // 2):
                at = g * (PER // 2) + k
                total = part_own[t, at, fsdp]
                for i in range(1, NZ):
                    total += z_in[t, g, (fsdp + NZ - i) % NZ, k].astype(F32)
                fin[t, at] = total
                to, src, dst, recv = fin_copy(t, at)

                @pl.when(to == clus)
                def _():
                    pltpu.make_async_copy(src, dst, recv).start()

                @pl.when(to != clus)
                def _():
                    remote(src, dst, fin_send.at[t, at], recv, (to, fsdp, clus // PER)).start()

    give.wait_send()
    for t in (0, 1):
        half_copy(t).wait_send()
        for g in (0, 1):

            @pl.loop(1, NZ)
            def _(i):
                z_copy(t, g, i).wait_send()

        for k in range(PER):
            to, src, dst, recv = fin_copy(t, k)

            @pl.when(to != clus)
            def _():
                remote(src, dst, fin_send.at[t, k], recv, (to, fsdp, clus // PER)).wait_send()

    @pl.loop(0, NC)
    def _(s):
        @pl.when(jnp.logical_not(jnp.logical_and(s == clus, own_out)))
        def _():
            out_copy(s).wait_send()

    for m in range(PER):
        for block in (0, 1):
            remote(
                out_blocks.at[0],
                out.at[pl.ds(block * BLK, BLK), pl.ds(m * HD, HD)],
                out_send.at[0],
                out_recv.at[2 * m + block],
                sibling,
            ).wait_recv()
        for t in (0, 1):
            remote(
                fin.at[t, 0],
                (grad_q, grad_k)[t].at[:, pl.ds(m * HD, HD)],
                fin_send.at[t, 0],
                fin_recv.at[t, m],
                sibling,
            ).wait_recv()


HB = pl.BlockSpec(memory_space=pltpu.HBM)
VM = pl.BlockSpec(memory_space=pltpu.VMEM)
SM = pl.BlockSpec(memory_space=pltpu.SMEM)
DMA = pltpu.SemaphoreType.DMA
MIB = 1 << 20


def shape(dims, kind):
    return jax.ShapeDtypeStruct(dims, kind)


def on_device(feats, w_query, w_keyval, grad_out, col_block, col_count):
    feats_all, query, keyval, cots = pl.pallas_call(
        gather_kernel,
        name="gather_project",
        out_shape=(
            shape((NC, BLK, D), BF),
            shape((NC, BLK, HD), BF),
            shape((2 * NC, 2, BLK, HD), BF),
            shape((NC, BLK, HD), BF),
        ),
        in_specs=[HB, VM, VM, HB],
        out_specs=(VM, VM, VM, VM),
        scratch_shapes=[
            pltpu.VMEM((2, WROWS, HALF), BF),
            pltpu.VMEM((2, NC, NZ, WROWS, HD), BF),
            DMA((40,)),
            DMA((40,)),
            DMA,
            DMA((16,)),
            DMA((NC,)),
            DMA((NZ,)),
            DMA((NZ,)),
            DMA,
            DMA,
            DMA((16,)),
            DMA((NC,)),
            DMA((NC,)),
            DMA((NC,)),
        ],
        compiler_params=pltpu.CompilerParams(
            collective_id=1, has_side_effects=True, vmem_limit_bytes=24 * MIB
        ),
        cost_estimate=pl.CostEstimate(
            flops=2 * D * D * 256, bytes_accessed=18 << 20, transcendentals=0
        ),
    )(feats, w_query, w_keyval, grad_out)
    out_blocks, dqt, dkv = pl.pallas_call(
        attend_kernel,
        name="attend",
        out_shape=(
            shape((NC, BLK, HD), BF),
            shape((HD, NC * BLK), BF),
            shape((NC, 2, BLK, HD), F32),
        ),
        in_specs=[VM, VM, VM, SM, SM],
        out_specs=(VM, VM, VM),
        compiler_params=pltpu.CompilerParams(vmem_limit_bytes=16 * MIB),
        cost_estimate=pl.CostEstimate(
            flops=12 * NC * BLK * 640 * HD, bytes_accessed=6 * MIB, transcendentals=NC * BLK * 640
        ),
    )(query, keyval, cots, col_block.T, col_count)
    return pl.pallas_call(
        scatter_kernel,
        name="scatter_grads",
        out_shape=(
            shape((2 * BLK, HALF), BF),
            shape((WROWS, HALF), F32),
            shape((WROWS, HALF), F32),
        ),
        in_specs=[VM, VM, VM, VM],
        out_specs=(VM, VM, VM),
        scratch_shapes=[
            pltpu.VMEM((NC, BLK, HD), F32),
            pltpu.VMEM((HD, NC * BLK), BF),
            pltpu.VMEM((2, PER, NZ, WROWS, HD), BF),
            pltpu.VMEM((2, PER, NZ, WROWS, HD), BF),
            pltpu.VMEM((2, PER, NZ, WROWS, HD), F32),
            pltpu.VMEM((2, 2, NZ, PER // 2, WROWS, HD), BF),
            pltpu.VMEM((2, 2, NZ, PER // 2, WROWS, HD), BF),
            pltpu.VMEM((2, PER, WROWS, HD), F32),
            DMA((2,)),
            DMA((NC,)),
            DMA((NC,)),
            DMA((2,)),
            DMA((2,)),
            DMA((4, NZ)),
            DMA((4, NZ)),
            DMA((2, PER)),
            DMA((2, PER)),
        ],
        compiler_params=pltpu.CompilerParams(
            collective_id=2, has_side_effects=True, vmem_limit_bytes=24 * MIB
        ),
        cost_estimate=pl.CostEstimate(
            flops=2 * D * D * 256, bytes_accessed=12 * MIB, transcendentals=0
        ),
    )(feats_all, out_blocks, dqt, dkv)


def solution(mesh):
    return jax.shard_map(
        on_device,
        mesh=mesh,
        in_specs=(
            P(("clus", "fsdp"), None),
            P(("clus", "fsdp"), "head"),
            P(("clus", "fsdp"), "head"),
            P(("clus", "fsdp"), "head"),
            P(),
            P(),
        ),
        out_specs=(
            P(("clus", "fsdp"), "head"),
            P(("clus", "fsdp"), "head"),
            P(("clus", "fsdp"), "head"),
        ),
        check_vma=False,
    )
```

```python
import functools
import math

import jax
import jax.numpy as jnp
from jax import lax
from jax.experimental import pallas as pl
from jax.experimental.pallas import tpu as pltpu
from jax.sharding import PartitionSpec as P

D = 2048
HD = 128
BLK = 128
NCOL = 5
SIDE = 4
NC = 16
NZ = 8
HALF = 1024
PER = 8
WROWS = 16
SCALE = 1.0 / math.sqrt(HD)
LOG2 = SCALE / math.log(2.0)
BF = jnp.bfloat16
F32 = jnp.float32
NT = (((1,), (1,)), ((), ()))
NN = (((1,), (0,)), ((), ()))


def here():
    return lax.axis_index("clus"), lax.axis_index("fsdp"), lax.axis_index("head")


def remote(src, dst, send, recv, device):
    return pltpu.make_async_remote_copy(
        src_ref=src,
        dst_ref=dst,
        send_sem=send,
        recv_sem=recv,
        device_id=device,
        device_id_type=pl.DeviceIdType.MESH,
    )


def greet(clus, fsdp, core):
    barrier = pltpu.get_barrier_semaphore()

    @pl.loop(0, NC)
    def _(i):
        for side in (0, 1):

            @pl.when(jnp.logical_or(i != clus, side != core))
            def _():
                pl.semaphore_signal(
                    barrier, inc=1, device_id=(i, fsdp, side), device_id_type=pl.DeviceIdType.MESH
                )

    @pl.loop(1, NZ)
    def _(i):
        pl.semaphore_signal(
            barrier,
            inc=1,
            device_id=(clus, (fsdp + i) % NZ, core),
            device_id_type=pl.DeviceIdType.MESH,
        )


def greeted():
    pl.semaphore_wait(pltpu.get_barrier_semaphore(), 2 * NC - 1 + NZ - 1)


def gather_kernel(
    feats,
    w_query,
    w_keyval,
    grad_out,
    rows,
    q_out,
    kv_out,
    cot_out,
    wf,
    wb,
    wall,
    wf_sem,
    ring_send,
    ring_recv,
    local_sem,
    col_send,
    col_recv,
    z_send,
    z_recv,
    swap_send,
    swap_recv,
    cot_send,
    cot_recv,
    kv_send,
    kv_recv,
):
    clus, fsdp, core = here()
    xp, yp = clus % SIDE, clus // SIDE

    def at(dx, dy):
        return ((yp + dy) % SIDE) * SIDE + (xp + dx) % SIDE

    loads = [
        pltpu.make_async_copy(w, wf.at[part], wf_sem.at[part])
        for part, w in enumerate((w_query, w_keyval))
    ]
    for load in loads:
        load.start()
    greet(clus, fsdp, core)
    for part, load in enumerate(loads):
        load.wait()
        wb[part] = wf[part].astype(BF)
    greeted()

    def slot(half, first, second):
        return at(first, second) if half == 0 else at(second, first)

    def hop(half, axis, step):
        return slot(half, step, 0) if axis == 0 else slot(half, 0, step)

    def ring(half, label, src, part, own):
        index = half * 20 + label
        axis = 0 if label < 4 else 1
        step = 1 if label % 2 == 0 else -1
        start = half * 64 + (32 if part == 2 else 0)
        count = 64 if part == 0 else 32
        if own:
            source = feats.at[pl.ds(pl.multiple_of(core * BLK, BLK) + start, count)]
        else:
            source = rows.at[src, pl.ds(start, count)]
        return remote(
            source,
            rows.at[src, pl.ds(start, count)],
            ring_send.at[index],
            ring_recv.at[index],
            (hop(half, axis, step), fsdp, core),
        )

    OFF = (0, -1, 1, 2)
    plan = {}
    for half in (0, 1):
        plan[half, 0] = (slot(half, 0, 0), slot(half, -1, 0), 0)
        plan[half, 1] = (slot(half, 0, 0), slot(half, 1, 0), 0)
        plan[half, 2] = (slot(half, -1, 0), slot(half, -2, 0), 1)
        plan[half, 3] = (slot(half, 1, 0), slot(half, 2, 0), 2)
        for k, o in enumerate(OFF):
            base = 4 + 4 * k
            plan[half, base] = (slot(half, o, 0), slot(half, o, -1), 0)
            plan[half, base + 1] = (slot(half, o, 0), slot(half, o, 1), 0)
            plan[half, base + 2] = (slot(half, o, -1), slot(half, o, -2), 1)
            plan[half, base + 3] = (slot(half, o, 1), slot(half, o, 2), 2)

    def send(*labels):
        for label in labels:
            for half in (0, 1):
                src, _, part = plan[half, label]
                ring(half, label, src, part, label in (0, 1, 4, 5)).start()

    def arrived(*labels):
        for label in labels:
            for half in (0, 1):
                _, dst, part = plan[half, label]
                ring(half, label, dst, part, False).wait_recv()

    send(0, 1)

    def column_copy(j, part):
        head = core * PER + j
        src = wb.at[part, :, pl.ds(pl.multiple_of(j * HD, HD), HD)]
        dst = wall.at[part, clus, fsdp]
        return head, src, dst

    @pl.loop(0, PER)
    def _(i):
        j = (i + clus) % PER
        for part in (0, 1):
            head, src, dst = column_copy(j, part)
            mine = jnp.logical_and(head == clus, core == part)

            @pl.when(mine)
            def _():
                pltpu.make_async_copy(src, dst, col_recv.at[clus]).start()

            @pl.when(jnp.logical_not(mine))
            def _():
                remote(
                    src, dst, col_send.at[2 * j + part], col_recv.at[clus], (head, fsdp, part)
                ).start()

    own_rows = pltpu.make_async_copy(
        feats.at[pl.ds(pl.multiple_of(core * BLK, BLK), BLK)], rows.at[clus], local_sem
    )
    own_rows.start()
    send(4, 5)

    @pl.loop(0, NC)
    def _(i):
        remote(
            wb.at[0, :, pl.ds(0, HD)],
            wall.at[core, i, fsdp],
            col_send.at[0],
            col_recv.at[i],
            (clus, fsdp, 1 - core),
        ).wait_recv()

    def z_copy(i):
        other = (fsdp + i) % NZ
        return remote(
            wall.at[core, :, fsdp],
            wall.at[core, :, fsdp],
            z_send.at[i],
            z_recv.at[i],
            (clus, other, core),
        )

    @pl.loop(1, NZ)
    def _(i):
        z_copy(i).start()

    def cot_copy(j, block):
        head = core * PER + j
        src = grad_out.at[
            pl.ds(block * BLK, BLK), pl.ds(pl.multiple_of(j * HD, HD), HD)
        ]
        return head, src, cot_out.at[clus]

    arrived(0, 1)
    send(2, 3, 8, 9, 12, 13)

    @pl.loop(0, PER)
    def _(i):
        j = (i + clus) % PER
        for block in (0, 1):
            head, src, dst = cot_copy(j, block)
            mine = jnp.logical_and(head == clus, core == block)

            @pl.when(mine)
            def _():
                pltpu.make_async_copy(src, dst, cot_recv.at[clus]).start()

            @pl.when(jnp.logical_not(mine))
            def _():
                remote(
                    src, dst, cot_send.at[2 * j + block], cot_recv.at[clus], (head, fsdp, block)
                ).start()


    @pl.loop(1, NZ)
    def _(i):
        other = (fsdp + NZ - i) % NZ
        remote(
            wall.at[core, :, other],
            wall.at[core, :, other],
            z_send.at[i],
            z_recv.at[i],
            (clus, other, core),
        ).wait_recv()

    swap = remote(
        wall.at[core], wall.at[core], swap_send, swap_recv, (clus, fsdp, 1 - core)
    )
    swap.start()
    arrived(4, 5)
    send(6, 7)
    arrived(2, 3)
    send(16, 17)
    remote(
        wall.at[1 - core], wall.at[1 - core], swap_send, swap_recv, (clus, fsdp, 1 - core)
    ).wait_recv()
    own_rows.wait()

    shared = []

    def project(dx, dy):
        src = at(dx, dy)
        index = len(shared)
        weights = jnp.concatenate(
            [wall[0].reshape(D, HD), wall[1].reshape(D, HD)], axis=1
        )
        both = lax.dot_general(rows[src], weights, NN, preferred_element_type=F32)
        q_out[src] = both[:, :HD].astype(BF)
        keys = both[:, HD:]
        mine = 2 * src + core
        kv_out[mine, 0] = keys.astype(BF)
        kv_out[mine, 1] = keys.T.astype(BF)
        share = remote(
            kv_out.at[mine],
            kv_out.at[mine],
            kv_send.at[index],
            kv_recv.at[index],
            (clus, fsdp, 1 - core),
        )
        share.start()
        theirs = 2 * src + 1 - core
        shared.append(
            (
                share,
                remote(
                    kv_out.at[theirs],
                    kv_out.at[theirs],
                    kv_send.at[index],
                    kv_recv.at[index],
                    (clus, fsdp, 1 - core),
                ),
            )
        )

    project(0, 0)
    arrived(8, 9, 12, 13)
    send(10, 11, 14, 15)
    project(1, 0)
    project(-1, 0)
    project(0, 1)
    arrived(16, 17)
    send(18, 19)
    project(0, -1)
    project(1, 1)
    project(-1, 1)
    project(1, -1)
    project(-1, -1)
    arrived(6, 7)
    project(2, 0)
    project(0, 2)
    arrived(10, 11, 14, 15)
    project(2, 1)
    project(2, -1)
    project(1, 2)
    project(-1, 2)
    arrived(18, 19)
    project(2, 2)

    @pl.loop(0, NC)
    def _(i):
        remote(
            grad_out.at[pl.ds(0, BLK), pl.ds(0, HD)],
            cot_out.at[i],
            cot_send.at[0],
            cot_recv.at[i],
            (clus, fsdp, 1 - core),
        ).wait_recv()

    @pl.loop(0, PER)
    def _(j):
        for part in (0, 1):
            head, src, dst = column_copy(j, part)
            _, csrc, cdst = cot_copy(j, part)

            @pl.when(jnp.logical_not(jnp.logical_and(head == clus, core == part)))
            def _():
                remote(
                    src, dst, col_send.at[2 * j + part], col_recv.at[clus], (head, fsdp, part)
                ).wait_send()
                remote(
                    csrc, cdst, cot_send.at[2 * j + part], cot_recv.at[clus], (head, fsdp, part)
                ).wait_send()

    @pl.loop(1, NZ)
    def _(i):
        z_copy(i).wait_send()

    swap.wait_send()
    for label in range(20):
        for half in (0, 1):
            src, _, part = plan[half, label]
            ring(half, label, src, part, label in (0, 1, 4, 5)).wait_send()
    for share, theirs in shared:
        share.wait_send()
        theirs.wait_recv()


def attend_kernel(q, kv, cot, col_block, col_count, out, dqt, total):
    clus, fsdp, core = here()
    total[...] = jnp.zeros_like(total)

    def stage_one(i):
        block = 2 * NZ * i + 2 * fsdp + core
        cols = [col_block[k, block] for k in range(NCOL)]
        cols = [(c // (2 * NZ)) * 2 + c % 2 for c in cols]
        live = col_count[block] == NCOL
        query, grad = q[i], cot[i]
        pair = jnp.concatenate([query, grad], axis=0)
        both = [
            lax.dot_general(kv[c, 0], pair, NT, preferred_element_type=F32) for c in cols
        ]
        return cols, live, query, grad, both

    def stage_two(cols, live, query, grad, both):
        scores = [x[:, :BLK] for x in both]
        scores[-1] = jnp.where(live, scores[-1], -1e30)
        top = functools.reduce(jnp.maximum, scores)
        top = jnp.max(top, axis=0, keepdims=True)
        expos = [jnp.exp2((x - top) * LOG2) for x in scores]
        norm = jnp.sum(functools.reduce(jnp.add, expos), axis=0, keepdims=True)
        inv = 1.0 / norm
        probs = [x * inv for x in expos]
        delta = functools.reduce(jnp.add, [p * x[:, BLK:] for p, x in zip(probs, both)])
        delta = jnp.sum(delta, axis=0, keepdims=True)
        ds = [(p * SCALE * (x[:, BLK:] - delta)).astype(BF) for p, x in zip(probs, both)]
        return ds, [p.astype(BF) for p in probs]

    def stage_three(i, cols, query, grad, ds, pb):
        keys_t = jnp.concatenate([kv[c, 1] for c in cols], axis=1)
        right = jnp.concatenate(
            [jnp.concatenate(ds, axis=0), jnp.concatenate(pb, axis=0)], axis=1
        )
        both_t = lax.dot_general(keys_t, right, NN, preferred_element_type=F32)
        dqt[:, pl.ds(pl.multiple_of(i * BLK, BLK), BLK)] = both_t[:, :BLK].astype(BF)
        out[i] = both_t[:, BLK:].T.astype(BF)
        pair = jnp.concatenate([query, grad], axis=0)
        for k, c in enumerate(cols):
            total[c // 2, c % 2] += lax.dot_general(
                jnp.concatenate([ds[k], pb[k]], axis=1), pair, NN, preferred_element_type=F32
            )

    GROUP = 4

    def step(n, carry):
        items = [n * GROUP + g for g in range(GROUP)]
        ones = [stage_one(i) for i in items]
        twos = [stage_two(*o) for o in ones]
        for i, o, t in zip(items, ones, twos):
            stage_three(i, o[0], o[2], o[3], *t)
        return carry

    lax.fori_loop(0, NC // GROUP, step, 0)


def scatter_kernel(
    feats,
    out_blocks,
    dqt,
    dkv,
    out,
    grad_q,
    grad_k,
    other,
    dkt,
    part_send,
    part_recv,
    part_own,
    z_out,
    z_in,
    fin,
    dk_sem,
    out_send,
    out_recv,
    half_send,
    half_recv,
    z_send,
    z_recv,
    fin_send,
    fin_recv,
):
    clus, fsdp, core = here()
    greet(clus, fsdp, core)
    sibling = (clus, fsdp, 1 - core)
    give = remote(dkv.at[:, 1 - core], other, dk_sem.at[0], dk_sem.at[1], sibling)

    def out_spot():
        return out.at[
            pl.ds(pl.multiple_of(core * BLK, BLK), BLK),
            pl.ds(pl.multiple_of((clus % PER) * HD, HD), HD),
        ]

    def out_copy(s):
        return remote(
            out_blocks.at[s],
            out_spot(),
            out_send.at[s],
            out_recv.at[2 * (clus % PER) + core],
            (s, fsdp, clus // PER),
        )

    own_out = core == clus // PER

    def send_out():
        @pl.loop(0, NC)
        def _(i):
            s = (i + clus) % NC
            mine = jnp.logical_and(s == clus, own_out)

            @pl.when(mine)
            def _():
                pltpu.make_async_copy(
                    out_blocks.at[s], out_spot(), out_recv.at[2 * (clus % PER) + core]
                ).start()

            @pl.when(jnp.logical_not(mine))
            def _():
                out_copy(s).start()

    def half_copy(t):
        return remote(
            part_send.at[t], part_recv.at[t], half_send.at[t], half_recv.at[t], sibling
        )

    HOPS = ((-2, -4), (-1, -3), (1, 3), (-1, -1), (1, 1), (-2, -2), (2, 2))

    def turn(t, steps):
        return (fsdp + NZ + (steps if t == 0 else -steps)) % NZ

    def z_copy(t, i):
        hops, owner = HOPS[i]
        return remote(
            z_out.at[t, turn(t, owner)],
            z_in.at[t, i],
            z_send.at[t, i],
            z_recv.at[t, i],
            (clus, turn(t, hops), core),
        )

    def stage_one(t):
        for i in range(5):
            z_copy(t, i).start()

    def stage_two(t):
        for i in range(3):
            z_copy(t, i).wait_recv()
        down, up = turn(t, -2), turn(t, 2)
        for k in range(PER):
            total = part_own[t, k, down] + z_in[t, 0, k].astype(F32) + z_in[t, 1, k].astype(F32)
            z_out[t, down, k] = total.astype(BF)
        z_copy(t, 5).start()
        for k in range(PER):
            z_out[t, up, k] = (part_own[t, k, up] + z_in[t, 2, k].astype(F32)).astype(BF)
        z_copy(t, 6).start()

    CH = 2 * BLK

    def chunk(lhs, n, side):
        cols = pl.ds(pl.multiple_of(side * HALF + n * CH, CH), CH)
        part = lax.dot_general(
            lhs[...],
            feats[:, :, cols].reshape(NC * BLK, CH),
            NN,
            preferred_element_type=F32,
        )
        return [part[:, k * BLK : (k + 1) * BLK].T.reshape(NZ, WROWS, HD) for k in (0, 1)]

    def for_sibling(t, lhs):
        for n in range(PER // 2):
            for k, piece in enumerate(chunk(lhs, n, 1 - core)):
                part_send[t, 2 * n + k] = piece.astype(BF)

    def for_self(t, lhs):
        for n in range(PER // 2):
            for k, piece in enumerate(chunk(lhs, n, core)):
                part_own[t, 2 * n + k] = piece

    def add_sibling(t):
        half_copy(t).wait_recv()
        for k in range(PER):
            total = part_own[t, k] + part_recv[t, k].astype(F32)
            part_own[t, k] = total
            z_out[t, :, k] = total.astype(BF)
        stage_one(t)

    for_sibling(0, dqt)
    for_self(0, dqt)
    greeted()
    half_copy(0).start()
    give.start()
    send_out()
    add_sibling(0)
    give.wait_recv()
    for s in range(NC):
        total = (dkv[s, core] + other[s]).astype(BF).astype(F32)
        dkt[:, s * BLK : (s + 1) * BLK] = total.T.astype(BF)
    for_sibling(1, dkt)
    half_copy(1).start()
    for_self(1, dkt)
    add_sibling(1)
    stage_two(0)
    stage_two(1)

    def fin_copy(t, k):
        dest = (grad_q, grad_k)[t]
        to = core * PER + k
        return (
            to,
            fin.at[t, k],
            dest.at[:, pl.ds(pl.multiple_of((clus % PER) * HD, HD), HD)],
            fin_recv.at[t, clus % PER],
        )

    for t in (0, 1):
        for i in range(3, 7):
            z_copy(t, i).wait_recv()
        for k in range(PER):
            total = part_own[t, k, fsdp]
            for i in range(3, 7):
                total += z_in[t, i, k].astype(F32)
            fin[t, k] = total

        @pl.loop(0, PER)
        def _(i):
            k = (i + clus) % PER
            to, src, dst, recv = fin_copy(t, k)

            @pl.when(to == clus)
            def _():
                pltpu.make_async_copy(src, dst, recv).start()

            @pl.when(to != clus)
            def _():
                remote(src, dst, fin_send.at[t, k], recv, (to, fsdp, clus // PER)).start()

    give.wait_send()
    for t in (0, 1):
        half_copy(t).wait_send()
        for i in range(7):
            z_copy(t, i).wait_send()


        @pl.loop(0, PER)
        def _(k):
            to, src, dst, recv = fin_copy(t, k)

            @pl.when(to != clus)
            def _():
                remote(src, dst, fin_send.at[t, k], recv, (to, fsdp, clus // PER)).wait_send()

    @pl.loop(0, NC)
    def _(s):
        @pl.when(jnp.logical_not(jnp.logical_and(s == clus, own_out)))
        def _():
            out_copy(s).wait_send()

    for m in range(PER):
        for block in (0, 1):
            remote(
                out_blocks.at[0],
                out.at[pl.ds(block * BLK, BLK), pl.ds(m * HD, HD)],
                out_send.at[0],
                out_recv.at[2 * m + block],
                sibling,
            ).wait_recv()
        for t in (0, 1):
            remote(
                fin.at[t, 0],
                (grad_q, grad_k)[t].at[:, pl.ds(m * HD, HD)],
                fin_send.at[t, 0],
                fin_recv.at[t, m],
                sibling,
            ).wait_recv()


def place_kernel(*refs):
    copies = [
        pltpu.make_async_copy(refs[i], refs[3 + i], refs[6].at[i]) for i in range(3)
    ]
    for copy in copies:
        copy.start()
    for copy in copies:
        copy.wait()


HB = pl.BlockSpec(memory_space=pltpu.HBM)
VM = pl.BlockSpec(memory_space=pltpu.VMEM)
SM = pl.BlockSpec(memory_space=pltpu.SMEM)
DMA = pltpu.SemaphoreType.DMA
MIB = 1 << 20


def shape(dims, kind):
    return jax.ShapeDtypeStruct(dims, kind)


def on_device(feats, w_query, w_keyval, grad_out, col_block, col_count):
    feats_all, query, keyval, cots = pl.pallas_call(
        gather_kernel,
        name="gather_project",
        out_shape=(
            shape((NC, BLK, D), BF),
            shape((NC, BLK, HD), BF),
            shape((2 * NC, 2, BLK, HD), BF),
            shape((NC, BLK, HD), BF),
        ),
        in_specs=[HB, HB, HB, HB],
        out_specs=(VM, VM, VM, VM),
        scratch_shapes=[
            pltpu.VMEM((2, WROWS, HALF), F32),
            pltpu.VMEM((2, WROWS, HALF), BF),
            pltpu.VMEM((2, NC, NZ, WROWS, HD), BF),
            DMA((2,)),
            DMA((40,)),
            DMA((40,)),
            DMA,
            DMA((16,)),
            DMA((NC,)),
            DMA((NZ,)),
            DMA((NZ,)),
            DMA,
            DMA,
            DMA((16,)),
            DMA((NC,)),
            DMA((NC,)),
            DMA((NC,)),
        ],
        compiler_params=pltpu.CompilerParams(
            collective_id=1, has_side_effects=True, vmem_limit_bytes=24 * MIB
        ),
        cost_estimate=pl.CostEstimate(
            flops=2 * D * D * 256, bytes_accessed=18 << 20, transcendentals=0
        ),
    )(*(pltpu.with_memory_space_constraint(x, pltpu.HBM) for x in (feats, w_query, w_keyval, grad_out)))
    out_blocks, dqt, dkv = pl.pallas_call(
        attend_kernel,
        name="attend",
        out_shape=(
            shape((NC, BLK, HD), BF),
            shape((HD, NC * BLK), BF),
            shape((NC, 2, BLK, HD), F32),
        ),
        in_specs=[VM, VM, VM, SM, SM],
        out_specs=(VM, VM, VM),
        compiler_params=pltpu.CompilerParams(vmem_limit_bytes=16 * MIB),
        cost_estimate=pl.CostEstimate(
            flops=12 * NC * BLK * 640 * HD, bytes_accessed=6 * MIB, transcendentals=NC * BLK * 640
        ),
    )(query, keyval, cots, col_block.T, col_count)
    results = pl.pallas_call(
        scatter_kernel,
        name="scatter_grads",
        out_shape=(
            shape((2 * BLK, HALF), BF),
            shape((WROWS, HALF), F32),
            shape((WROWS, HALF), F32),
        ),
        in_specs=[VM, VM, VM, VM],
        out_specs=(VM, VM, VM),
        scratch_shapes=[
            pltpu.VMEM((NC, BLK, HD), F32),
            pltpu.VMEM((HD, NC * BLK), BF),
            pltpu.VMEM((2, PER, NZ, WROWS, HD), BF),
            pltpu.VMEM((2, PER, NZ, WROWS, HD), BF),
            pltpu.VMEM((2, PER, NZ, WROWS, HD), F32),
            pltpu.VMEM((2, NZ, PER, WROWS, HD), BF),
            pltpu.VMEM((2, 7, PER, WROWS, HD), BF),
            pltpu.VMEM((2, PER, WROWS, HD), F32),
            DMA((2,)),
            DMA((NC,)),
            DMA((NC,)),
            DMA((2,)),
            DMA((2,)),
            DMA((2, 7)),
            DMA((2, 7)),
            DMA((2, PER)),
            DMA((2, PER)),
        ],
        compiler_params=pltpu.CompilerParams(
            collective_id=2, has_side_effects=True, vmem_limit_bytes=24 * MIB
        ),
        cost_estimate=pl.CostEstimate(
            flops=2 * D * D * 256, bytes_accessed=12 * MIB, transcendentals=0
        ),
    )(feats_all, out_blocks, dqt, dkv)
    return pl.pallas_call(
        place_kernel,
        name="place",
        out_shape=tuple(pltpu.HBM(r.shape, r.dtype) for r in results),
        in_specs=[VM] * 3,
        out_specs=(HB,) * 3,
        scratch_shapes=[DMA((3,))],
        compiler_params=pltpu.CompilerParams(vmem_limit_bytes=16 * MIB),
    )(*results)


def solution(mesh):
    return jax.shard_map(
        on_device,
        mesh=mesh,
        in_specs=(
            P(("clus", "fsdp"), None),
            P(("clus", "fsdp"), "head"),
            P(("clus", "fsdp"), "head"),
            P(("clus", "fsdp"), "head"),
            P(),
            P(),
        ),
        out_specs=(
            P(("clus", "fsdp"), "head"),
            P(("clus", "fsdp"), "head"),
            P(("clus", "fsdp"), "head"),
        ),
        check_vma=False,
    )
```

```python
import functools
import math

import jax
import jax.numpy as jnp
from jax import lax
from jax.experimental import pallas as pl
from jax.experimental.pallas import tpu as pltpu
from jax.sharding import PartitionSpec as P

D = 2048
HD = 128
BLK = 128
NCOL = 5
SIDE = 4
NC = 16
NZ = 8
HALF = 1024
PER = 8
WROWS = 16
SCALE = 1.0 / math.sqrt(HD)
LOG2 = SCALE / math.log(2.0)
BF = jnp.bfloat16
F32 = jnp.float32
NT = (((1,), (1,)), ((), ()))
NN = (((1,), (0,)), ((), ()))


def here():
    return lax.axis_index("clus"), lax.axis_index("fsdp"), lax.axis_index("head")


def remote(src, dst, send, recv, device):
    return pltpu.make_async_remote_copy(
        src_ref=src,
        dst_ref=dst,
        send_sem=send,
        recv_sem=recv,
        device_id=device,
        device_id_type=pl.DeviceIdType.MESH,
    )


def greet(clus, fsdp, core):
    barrier = pltpu.get_barrier_semaphore()

    @pl.loop(0, NC)
    def _(i):
        for side in (0, 1):

            @pl.when(jnp.logical_or(i != clus, side != core))
            def _():
                pl.semaphore_signal(
                    barrier, inc=1, device_id=(i, fsdp, side), device_id_type=pl.DeviceIdType.MESH
                )

    @pl.loop(1, NZ)
    def _(i):
        pl.semaphore_signal(
            barrier,
            inc=1,
            device_id=(clus, (fsdp + i) % NZ, core),
            device_id_type=pl.DeviceIdType.MESH,
        )


def greeted():
    pl.semaphore_wait(pltpu.get_barrier_semaphore(), 2 * NC - 1 + NZ - 1)


def gather_kernel(
    feats,
    w_query,
    w_keyval,
    grad_out,
    rows,
    q_out,
    kv_out,
    cot_out,
    wf,
    wb,
    wall,
    wf_sem,
    ring_send,
    ring_recv,
    local_sem,
    col_send,
    col_recv,
    z_send,
    z_recv,
    swap_send,
    swap_recv,
    cot_send,
    cot_recv,
    kv_send,
    kv_recv,
):
    clus, fsdp, core = here()
    xp, yp = clus % SIDE, clus // SIDE

    def at(dx, dy):
        return ((yp + dy) % SIDE) * SIDE + (xp + dx) % SIDE

    loads = [
        pltpu.make_async_copy(w, wf.at[part], wf_sem.at[part])
        for part, w in enumerate((w_query, w_keyval))
    ]
    for load in loads:
        load.start()
    greet(clus, fsdp, core)
    for part, load in enumerate(loads):
        load.wait()
        wb[part] = wf[part].astype(BF)
    greeted()

    def slot(half, first, second):
        return at(first, second) if half == 0 else at(second, first)

    def hop(half, axis, step):
        return slot(half, step, 0) if axis == 0 else slot(half, 0, step)

    def ring(half, label, src, part, own):
        index = half * 20 + label
        axis = 0 if label < 4 else 1
        step = 1 if label % 2 == 0 else -1
        start = half * 64 + (32 if part == 2 else 0)
        count = 64 if part == 0 else 32
        if own:
            source = feats.at[pl.ds(pl.multiple_of(core * BLK, BLK) + start, count)]
        else:
            source = rows.at[src, pl.ds(start, count)]
        return remote(
            source,
            rows.at[src, pl.ds(start, count)],
            ring_send.at[index],
            ring_recv.at[index],
            (hop(half, axis, step), fsdp, core),
        )

    OFF = (0, -1, 1, 2)
    plan = {}
    for half in (0, 1):
        plan[half, 0] = (slot(half, 0, 0), slot(half, -1, 0), 0)
        plan[half, 1] = (slot(half, 0, 0), slot(half, 1, 0), 0)
        plan[half, 2] = (slot(half, -1, 0), slot(half, -2, 0), 1)
        plan[half, 3] = (slot(half, 1, 0), slot(half, 2, 0), 2)
        for k, o in enumerate(OFF):
            base = 4 + 4 * k
            plan[half, base] = (slot(half, o, 0), slot(half, o, -1), 0)
            plan[half, base + 1] = (slot(half, o, 0), slot(half, o, 1), 0)
            plan[half, base + 2] = (slot(half, o, -1), slot(half, o, -2), 1)
            plan[half, base + 3] = (slot(half, o, 1), slot(half, o, 2), 2)

    def send(*labels):
        for label in labels:
            for half in (0, 1):
                src, _, part = plan[half, label]
                ring(half, label, src, part, label in (0, 1, 4, 5)).start()

    def arrived(*labels):
        for label in labels:
            for half in (0, 1):
                _, dst, part = plan[half, label]
                ring(half, label, dst, part, False).wait_recv()

    send(0, 1)

    def column_copy(j, part):
        head = core * PER + j
        src = wb.at[part, :, pl.ds(pl.multiple_of(j * HD, HD), HD)]
        dst = wall.at[part, clus, fsdp]
        return head, src, dst

    @pl.loop(0, PER)
    def _(i):
        j = (i + clus) % PER
        for part in (0, 1):
            head, src, dst = column_copy(j, part)
            mine = jnp.logical_and(head == clus, core == part)

            @pl.when(mine)
            def _():
                pltpu.make_async_copy(src, dst, col_recv.at[clus]).start()

            @pl.when(jnp.logical_not(mine))
            def _():
                remote(
                    src, dst, col_send.at[2 * j + part], col_recv.at[clus], (head, fsdp, part)
                ).start()

    own_rows = pltpu.make_async_copy(
        feats.at[pl.ds(pl.multiple_of(core * BLK, BLK), BLK)], rows.at[clus], local_sem
    )
    own_rows.start()
    send(4, 5)

    @pl.loop(0, NC)
    def _(i):
        remote(
            wb.at[0, :, pl.ds(0, HD)],
            wall.at[core, i, fsdp],
            col_send.at[0],
            col_recv.at[i],
            (clus, fsdp, 1 - core),
        ).wait_recv()

    def z_copy(i):
        other = (fsdp + i) % NZ
        return remote(
            wall.at[core, :, fsdp],
            wall.at[core, :, fsdp],
            z_send.at[i],
            z_recv.at[i],
            (clus, other, core),
        )

    @pl.loop(1, NZ)
    def _(i):
        z_copy(i).start()

    def cot_copy(j, block):
        head = core * PER + j
        src = grad_out.at[
            pl.ds(block * BLK, BLK), pl.ds(pl.multiple_of(j * HD, HD), HD)
        ]
        return head, src, cot_out.at[clus]

    arrived(0, 1)
    send(2, 3, 8, 9, 12, 13)

    @pl.loop(0, PER)
    def _(i):
        j = (i + clus) % PER
        for block in (0, 1):
            head, src, dst = cot_copy(j, block)
            mine = jnp.logical_and(head == clus, core == block)

            @pl.when(mine)
            def _():
                pltpu.make_async_copy(src, dst, cot_recv.at[clus]).start()

            @pl.when(jnp.logical_not(mine))
            def _():
                remote(
                    src, dst, cot_send.at[2 * j + block], cot_recv.at[clus], (head, fsdp, block)
                ).start()


    @pl.loop(1, NZ)
    def _(i):
        other = (fsdp + NZ - i) % NZ
        remote(
            wall.at[core, :, other],
            wall.at[core, :, other],
            z_send.at[i],
            z_recv.at[i],
            (clus, other, core),
        ).wait_recv()

    swap = remote(
        wall.at[core], wall.at[core], swap_send, swap_recv, (clus, fsdp, 1 - core)
    )
    swap.start()
    arrived(4, 5)
    send(6, 7)
    arrived(2, 3)
    send(16, 17)
    remote(
        wall.at[1 - core], wall.at[1 - core], swap_send, swap_recv, (clus, fsdp, 1 - core)
    ).wait_recv()
    own_rows.wait()

    shared = []

    def project(dx, dy):
        src = at(dx, dy)
        index = len(shared)
        weights = jnp.concatenate(
            [wall[0].reshape(D, HD), wall[1].reshape(D, HD)], axis=1
        )
        both = lax.dot_general(rows[src], weights, NN, preferred_element_type=F32)
        q_out[src] = both[:, :HD].astype(BF)
        keys = both[:, HD:]
        mine = 2 * src + core
        kv_out[mine, 0] = keys.astype(BF)
        kv_out[mine, 1] = keys.T.astype(BF)
        share = remote(
            kv_out.at[mine],
            kv_out.at[mine],
            kv_send.at[index],
            kv_recv.at[index],
            (clus, fsdp, 1 - core),
        )
        share.start()
        theirs = 2 * src + 1 - core
        shared.append(
            (
                share,
                remote(
                    kv_out.at[theirs],
                    kv_out.at[theirs],
                    kv_send.at[index],
                    kv_recv.at[index],
                    (clus, fsdp, 1 - core),
                ),
            )
        )

    project(0, 0)
    arrived(8, 9, 12, 13)
    send(10, 11, 14, 15)
    project(1, 0)
    project(-1, 0)
    project(0, 1)
    arrived(16, 17)
    send(18, 19)
    project(0, -1)
    project(1, 1)
    project(-1, 1)
    project(1, -1)
    project(-1, -1)
    arrived(6, 7)
    project(2, 0)
    project(0, 2)
    arrived(10, 11, 14, 15)
    project(2, 1)
    project(2, -1)
    project(1, 2)
    project(-1, 2)
    arrived(18, 19)
    project(2, 2)

    @pl.loop(0, NC)
    def _(i):
        remote(
            grad_out.at[pl.ds(0, BLK), pl.ds(0, HD)],
            cot_out.at[i],
            cot_send.at[0],
            cot_recv.at[i],
            (clus, fsdp, 1 - core),
        ).wait_recv()

    @pl.loop(0, PER)
    def _(j):
        for part in (0, 1):
            head, src, dst = column_copy(j, part)
            _, csrc, cdst = cot_copy(j, part)

            @pl.when(jnp.logical_not(jnp.logical_and(head == clus, core == part)))
            def _():
                remote(
                    src, dst, col_send.at[2 * j + part], col_recv.at[clus], (head, fsdp, part)
                ).wait_send()
                remote(
                    csrc, cdst, cot_send.at[2 * j + part], cot_recv.at[clus], (head, fsdp, part)
                ).wait_send()

    @pl.loop(1, NZ)
    def _(i):
        z_copy(i).wait_send()

    swap.wait_send()
    for label in range(20):
        for half in (0, 1):
            src, _, part = plan[half, label]
            ring(half, label, src, part, label in (0, 1, 4, 5)).wait_send()
    for share, theirs in shared:
        share.wait_send()
        theirs.wait_recv()


def attend_kernel(q, kv, cot, col_block, col_count, out, dqt, total):
    clus, fsdp, core = here()
    total[...] = jnp.zeros_like(total)

    def stage_one(i):
        block = 2 * NZ * i + 2 * fsdp + core
        cols = [col_block[k, block] for k in range(NCOL)]
        cols = [(c // (2 * NZ)) * 2 + c % 2 for c in cols]
        live = col_count[block] == NCOL
        query, grad = q[i], cot[i]
        pair = jnp.concatenate([query, grad], axis=0)
        both = [
            lax.dot_general(kv[c, 0], pair, NT, preferred_element_type=F32) for c in cols
        ]
        return cols, live, query, grad, both

    def stage_two(cols, live, query, grad, both):
        scores = [x[:, :BLK] for x in both]
        scores[-1] = jnp.where(live, scores[-1], -1e30)
        top = functools.reduce(jnp.maximum, scores)
        top = jnp.max(top, axis=0, keepdims=True)
        expos = [jnp.exp2((x - top) * LOG2) for x in scores]
        norm = jnp.sum(functools.reduce(jnp.add, expos), axis=0, keepdims=True)
        inv = 1.0 / norm
        probs = [x * inv for x in expos]
        delta = functools.reduce(jnp.add, [p * x[:, BLK:] for p, x in zip(probs, both)])
        delta = jnp.sum(delta, axis=0, keepdims=True)
        ds = [(p * SCALE * (x[:, BLK:] - delta)).astype(BF) for p, x in zip(probs, both)]
        return ds, [p.astype(BF) for p in probs]

    def stage_three(i, cols, query, grad, ds, pb):
        keys_t = jnp.concatenate([kv[c, 1] for c in cols], axis=1)
        right = jnp.concatenate(
            [jnp.concatenate(ds, axis=0), jnp.concatenate(pb, axis=0)], axis=1
        )
        both_t = lax.dot_general(keys_t, right, NN, preferred_element_type=F32)
        dqt[:, pl.ds(pl.multiple_of(i * BLK, BLK), BLK)] = both_t[:, :BLK].astype(BF)
        out[i] = both_t[:, BLK:].T.astype(BF)
        pair = jnp.concatenate([query, grad], axis=0)
        for k, c in enumerate(cols):
            total[c // 2, c % 2] += lax.dot_general(
                jnp.concatenate([ds[k], pb[k]], axis=1), pair, NN, preferred_element_type=F32
            )

    GROUP = 8

    def step(n, carry):
        items = [n * GROUP + g for g in range(GROUP)]
        ones = [stage_one(i) for i in items]
        twos = [stage_two(*o) for o in ones]
        for i, o, t in zip(items, ones, twos):
            stage_three(i, o[0], o[2], o[3], *t)
        return carry

    lax.fori_loop(0, NC // GROUP, step, 0)


def scatter_kernel(
    feats,
    out_blocks,
    dqt,
    dkv,
    out,
    grad_q,
    grad_k,
    other,
    dkt,
    part_send,
    part_recv,
    part_own,
    z_out,
    z_in,
    fin,
    dk_sem,
    out_send,
    out_recv,
    half_send,
    half_recv,
    z_send,
    z_recv,
    fin_send,
    fin_recv,
):
    clus, fsdp, core = here()
    greet(clus, fsdp, core)
    sibling = (clus, fsdp, 1 - core)
    give = remote(dkv.at[:, 1 - core], other, dk_sem.at[0], dk_sem.at[1], sibling)

    def out_spot():
        return out.at[
            pl.ds(pl.multiple_of(core * BLK, BLK), BLK),
            pl.ds(pl.multiple_of((clus % PER) * HD, HD), HD),
        ]

    def out_copy(s):
        return remote(
            out_blocks.at[s],
            out_spot(),
            out_send.at[s],
            out_recv.at[2 * (clus % PER) + core],
            (s, fsdp, clus // PER),
        )

    own_out = core == clus // PER

    def send_out():
        @pl.loop(0, NC)
        def _(i):
            s = (i + clus) % NC
            mine = jnp.logical_and(s == clus, own_out)

            @pl.when(mine)
            def _():
                pltpu.make_async_copy(
                    out_blocks.at[s], out_spot(), out_recv.at[2 * (clus % PER) + core]
                ).start()

            @pl.when(jnp.logical_not(mine))
            def _():
                out_copy(s).start()

    def half_copy(t):
        return remote(
            part_send.at[t], part_recv.at[t], half_send.at[t], half_recv.at[t], sibling
        )

    HOPS = ((-2, -4), (-1, -3), (1, 3), (-1, -1), (1, 1), (-2, -2), (2, 2))

    def turn(t, steps):
        return (fsdp + NZ + (steps if t == 0 else -steps)) % NZ

    def z_copy(t, i):
        hops, owner = HOPS[i]
        return remote(
            z_out.at[t, turn(t, owner)],
            z_in.at[t, i],
            z_send.at[t, i],
            z_recv.at[t, i],
            (clus, turn(t, hops), core),
        )

    def stage_one(t):
        for i in range(5):
            z_copy(t, i).start()

    def stage_two(t):
        for i in range(3):
            z_copy(t, i).wait_recv()
        down, up = turn(t, -2), turn(t, 2)
        for k in range(PER):
            total = part_own[t, k, down] + z_in[t, 0, k].astype(F32) + z_in[t, 1, k].astype(F32)
            z_out[t, down, k] = total.astype(BF)
        z_copy(t, 5).start()
        for k in range(PER):
            z_out[t, up, k] = (part_own[t, k, up] + z_in[t, 2, k].astype(F32)).astype(BF)
        z_copy(t, 6).start()

    CH = 2 * BLK

    def chunk(lhs, n, side):
        cols = pl.ds(pl.multiple_of(side * HALF + n * CH, CH), CH)
        part = lax.dot_general(
            lhs[...],
            feats[:, :, cols].reshape(NC * BLK, CH),
            NN,
            preferred_element_type=F32,
        )
        return [part[:, k * BLK : (k + 1) * BLK].T.reshape(NZ, WROWS, HD) for k in (0, 1)]

    def for_sibling(t, lhs):
        for n in range(PER // 2):
            for k, piece in enumerate(chunk(lhs, n, 1 - core)):
                part_send[t, 2 * n + k] = piece.astype(BF)

    def for_self(t, lhs):
        for n in range(PER // 2):
            for k, piece in enumerate(chunk(lhs, n, core)):
                part_own[t, 2 * n + k] = piece

    def add_sibling(t):
        half_copy(t).wait_recv()
        for k in range(PER):
            total = part_own[t, k] + part_recv[t, k].astype(F32)
            part_own[t, k] = total
            z_out[t, :, k] = total.astype(BF)
        stage_one(t)

    for_sibling(0, dqt)
    for_self(0, dqt)
    greeted()
    half_copy(0).start()
    give.start()
    send_out()
    add_sibling(0)
    give.wait_recv()
    for s in range(NC):
        total = (dkv[s, core] + other[s]).astype(BF).astype(F32)
        dkt[:, s * BLK : (s + 1) * BLK] = total.T.astype(BF)
    for_sibling(1, dkt)
    half_copy(1).start()
    for_self(1, dkt)
    add_sibling(1)
    stage_two(0)
    stage_two(1)

    def fin_copy(t, k):
        dest = (grad_q, grad_k)[t]
        to = core * PER + k
        return (
            to,
            fin.at[t, k],
            dest.at[:, pl.ds(pl.multiple_of((clus % PER) * HD, HD), HD)],
            fin_recv.at[t, clus % PER],
        )

    for t in (0, 1):
        for i in range(3, 7):
            z_copy(t, i).wait_recv()
        for k in range(PER):
            total = part_own[t, k, fsdp]
            for i in range(3, 7):
                total += z_in[t, i, k].astype(F32)
            fin[t, k] = total

        @pl.loop(0, PER)
        def _(i):
            k = (i + clus) % PER
            to, src, dst, recv = fin_copy(t, k)

            @pl.when(to == clus)
            def _():
                pltpu.make_async_copy(src, dst, recv).start()

            @pl.when(to != clus)
            def _():
                remote(src, dst, fin_send.at[t, k], recv, (to, fsdp, clus // PER)).start()

    give.wait_send()
    for t in (0, 1):
        half_copy(t).wait_send()
        for i in range(7):
            z_copy(t, i).wait_send()


        @pl.loop(0, PER)
        def _(k):
            to, src, dst, recv = fin_copy(t, k)

            @pl.when(to != clus)
            def _():
                remote(src, dst, fin_send.at[t, k], recv, (to, fsdp, clus // PER)).wait_send()

    @pl.loop(0, NC)
    def _(s):
        @pl.when(jnp.logical_not(jnp.logical_and(s == clus, own_out)))
        def _():
            out_copy(s).wait_send()

    for m in range(PER):
        for block in (0, 1):
            remote(
                out_blocks.at[0],
                out.at[pl.ds(block * BLK, BLK), pl.ds(m * HD, HD)],
                out_send.at[0],
                out_recv.at[2 * m + block],
                sibling,
            ).wait_recv()
        for t in (0, 1):
            remote(
                fin.at[t, 0],
                (grad_q, grad_k)[t].at[:, pl.ds(m * HD, HD)],
                fin_send.at[t, 0],
                fin_recv.at[t, m],
                sibling,
            ).wait_recv()


def place_kernel(*refs):
    copies = [
        pltpu.make_async_copy(refs[i], refs[3 + i], refs[6].at[i]) for i in range(3)
    ]
    for copy in copies:
        copy.start()
    for copy in copies:
        copy.wait()


HB = pl.BlockSpec(memory_space=pltpu.HBM)
VM = pl.BlockSpec(memory_space=pltpu.VMEM)
SM = pl.BlockSpec(memory_space=pltpu.SMEM)
DMA = pltpu.SemaphoreType.DMA
MIB = 1 << 20


def shape(dims, kind):
    return jax.ShapeDtypeStruct(dims, kind)


def on_device(feats, w_query, w_keyval, grad_out, col_block, col_count):
    feats_all, query, keyval, cots = pl.pallas_call(
        gather_kernel,
        name="gather_project",
        out_shape=(
            shape((NC, BLK, D), BF),
            shape((NC, BLK, HD), BF),
            shape((2 * NC, 2, BLK, HD), BF),
            shape((NC, BLK, HD), BF),
        ),
        in_specs=[HB, HB, HB, HB],
        out_specs=(VM, VM, VM, VM),
        scratch_shapes=[
            pltpu.VMEM((2, WROWS, HALF), F32),
            pltpu.VMEM((2, WROWS, HALF), BF),
            pltpu.VMEM((2, NC, NZ, WROWS, HD), BF),
            DMA((2,)),
            DMA((40,)),
            DMA((40,)),
            DMA,
            DMA((16,)),
            DMA((NC,)),
            DMA((NZ,)),
            DMA((NZ,)),
            DMA,
            DMA,
            DMA((16,)),
            DMA((NC,)),
            DMA((NC,)),
            DMA((NC,)),
        ],
        compiler_params=pltpu.CompilerParams(
            collective_id=1, has_side_effects=True, vmem_limit_bytes=24 * MIB
        ),
        cost_estimate=pl.CostEstimate(
            flops=2 * D * D * 256, bytes_accessed=18 << 20, transcendentals=0
        ),
    )(*(pltpu.with_memory_space_constraint(x, pltpu.HBM) for x in (feats, w_query, w_keyval, grad_out)))
    out_blocks, dqt, dkv = pl.pallas_call(
        attend_kernel,
        name="attend",
        out_shape=(
            shape((NC, BLK, HD), BF),
            shape((HD, NC * BLK), BF),
            shape((NC, 2, BLK, HD), F32),
        ),
        in_specs=[VM, VM, VM, SM, SM],
        out_specs=(VM, VM, VM),
        compiler_params=pltpu.CompilerParams(vmem_limit_bytes=16 * MIB),
        cost_estimate=pl.CostEstimate(
            flops=12 * NC * BLK * 640 * HD, bytes_accessed=6 * MIB, transcendentals=NC * BLK * 640
        ),
    )(query, keyval, cots, col_block.T, col_count)
    results = pl.pallas_call(
        scatter_kernel,
        name="scatter_grads",
        out_shape=(
            shape((2 * BLK, HALF), BF),
            shape((WROWS, HALF), F32),
            shape((WROWS, HALF), F32),
        ),
        in_specs=[VM, VM, VM, VM],
        out_specs=(VM, VM, VM),
        scratch_shapes=[
            pltpu.VMEM((NC, BLK, HD), F32),
            pltpu.VMEM((HD, NC * BLK), BF),
            pltpu.VMEM((2, PER, NZ, WROWS, HD), BF),
            pltpu.VMEM((2, PER, NZ, WROWS, HD), BF),
            pltpu.VMEM((2, PER, NZ, WROWS, HD), F32),
            pltpu.VMEM((2, NZ, PER, WROWS, HD), BF),
            pltpu.VMEM((2, 7, PER, WROWS, HD), BF),
            pltpu.VMEM((2, PER, WROWS, HD), F32),
            DMA((2,)),
            DMA((NC,)),
            DMA((NC,)),
            DMA((2,)),
            DMA((2,)),
            DMA((2, 7)),
            DMA((2, 7)),
            DMA((2, PER)),
            DMA((2, PER)),
        ],
        compiler_params=pltpu.CompilerParams(
            collective_id=2, has_side_effects=True, vmem_limit_bytes=24 * MIB
        ),
        cost_estimate=pl.CostEstimate(
            flops=2 * D * D * 256, bytes_accessed=12 * MIB, transcendentals=0
        ),
    )(feats_all, out_blocks, dqt, dkv)
    return pl.pallas_call(
        place_kernel,
        name="place",
        out_shape=tuple(pltpu.HBM(r.shape, r.dtype) for r in results),
        in_specs=[VM] * 3,
        out_specs=(HB,) * 3,
        scratch_shapes=[DMA((3,))],
        compiler_params=pltpu.CompilerParams(vmem_limit_bytes=16 * MIB),
    )(*results)


def solution(mesh):
    return jax.shard_map(
        on_device,
        mesh=mesh,
        in_specs=(
            P(("clus", "fsdp"), None),
            P(("clus", "fsdp"), "head"),
            P(("clus", "fsdp"), "head"),
            P(("clus", "fsdp"), "head"),
            P(),
            P(),
        ),
        out_specs=(
            P(("clus", "fsdp"), "head"),
            P(("clus", "fsdp"), "head"),
            P(("clus", "fsdp"), "head"),
        ),
        check_vma=False,
    )
```

```python
import functools
import math

import jax
import jax.numpy as jnp
from jax import lax
from jax.experimental import pallas as pl
from jax.experimental.pallas import tpu as pltpu
from jax.sharding import PartitionSpec as P

D = 2048
HD = 128
BLK = 128
NCOL = 5
SIDE = 4
NC = 16
NZ = 8
HALF = 1024
PER = 8
WROWS = 16
SCALE = 1.0 / math.sqrt(HD)
LOG2 = SCALE / math.log(2.0)
BF = jnp.bfloat16
F32 = jnp.float32
NT = (((1,), (1,)), ((), ()))
NN = (((1,), (0,)), ((), ()))


def here():
    return lax.axis_index("clus"), lax.axis_index("fsdp"), lax.axis_index("head")


def remote(src, dst, send, recv, device):
    return pltpu.make_async_remote_copy(
        src_ref=src,
        dst_ref=dst,
        send_sem=send,
        recv_sem=recv,
        device_id=device,
        device_id_type=pl.DeviceIdType.MESH,
    )


def greet(clus, fsdp, core):
    barrier = pltpu.get_barrier_semaphore()

    @pl.loop(0, NC)
    def _(i):
        for side in (0, 1):

            @pl.when(jnp.logical_or(i != clus, side != core))
            def _():
                pl.semaphore_signal(
                    barrier, inc=1, device_id=(i, fsdp, side), device_id_type=pl.DeviceIdType.MESH
                )

    @pl.loop(1, NZ)
    def _(i):
        pl.semaphore_signal(
            barrier,
            inc=1,
            device_id=(clus, (fsdp + i) % NZ, core),
            device_id_type=pl.DeviceIdType.MESH,
        )


def greeted():
    pl.semaphore_wait(pltpu.get_barrier_semaphore(), 2 * NC - 1 + NZ - 1)


def gather_kernel(
    feats,
    w_query,
    w_keyval,
    grad_out,
    rows,
    q_out,
    kv_out,
    cot_out,
    wf,
    wb,
    wall,
    wf_sem,
    ring_send,
    ring_recv,
    local_sem,
    col_send,
    col_recv,
    z_send,
    z_recv,
    swap_send,
    swap_recv,
    cot_send,
    cot_recv,
    kv_send,
    kv_recv,
):
    clus, fsdp, core = here()
    xp, yp = clus % SIDE, clus // SIDE

    def at(dx, dy):
        return ((yp + dy) % SIDE) * SIDE + (xp + dx) % SIDE

    loads = [
        pltpu.make_async_copy(w, wf.at[part], wf_sem.at[part])
        for part, w in enumerate((w_query, w_keyval))
    ]
    for load in loads:
        load.start()
    greet(clus, fsdp, core)
    for part, load in enumerate(loads):
        load.wait()
        wb[part] = wf[part].astype(BF)
    greeted()

    def slot(half, first, second):
        return at(first, second) if half == 0 else at(second, first)

    def hop(half, axis, step):
        return slot(half, step, 0) if axis == 0 else slot(half, 0, step)

    def ring(half, label, src, part, own):
        index = half * 20 + label
        axis = 0 if label < 4 else 1
        step = 1 if label % 2 == 0 else -1
        start = half * 64 + (32 if part == 2 else 0)
        count = 64 if part == 0 else 32
        if own:
            source = feats.at[pl.ds(pl.multiple_of(core * BLK, BLK) + start, count)]
        else:
            source = rows.at[src, pl.ds(start, count)]
        return remote(
            source,
            rows.at[src, pl.ds(start, count)],
            ring_send.at[index],
            ring_recv.at[index],
            (hop(half, axis, step), fsdp, core),
        )

    OFF = (0, -1, 1, 2)
    plan = {}
    for half in (0, 1):
        plan[half, 0] = (slot(half, 0, 0), slot(half, -1, 0), 0)
        plan[half, 1] = (slot(half, 0, 0), slot(half, 1, 0), 0)
        plan[half, 2] = (slot(half, -1, 0), slot(half, -2, 0), 1)
        plan[half, 3] = (slot(half, 1, 0), slot(half, 2, 0), 2)
        for k, o in enumerate(OFF):
            base = 4 + 4 * k
            plan[half, base] = (slot(half, o, 0), slot(half, o, -1), 0)
            plan[half, base + 1] = (slot(half, o, 0), slot(half, o, 1), 0)
            plan[half, base + 2] = (slot(half, o, -1), slot(half, o, -2), 1)
            plan[half, base + 3] = (slot(half, o, 1), slot(half, o, 2), 2)

    def send(*labels):
        for label in labels:
            for half in (0, 1):
                src, _, part = plan[half, label]
                ring(half, label, src, part, label in (0, 1, 4, 5)).start()

    def arrived(*labels):
        for label in labels:
            for half in (0, 1):
                _, dst, part = plan[half, label]
                ring(half, label, dst, part, False).wait_recv()

    send(0, 1)

    def column_copy(j, part):
        head = core * PER + j
        src = wb.at[part, :, pl.ds(pl.multiple_of(j * HD, HD), HD)]
        dst = wall.at[part, clus, fsdp]
        return head, src, dst

    @pl.loop(0, PER)
    def _(i):
        j = (i + clus) % PER
        for part in (0, 1):
            head, src, dst = column_copy(j, part)
            mine = jnp.logical_and(head == clus, core == part)

            @pl.when(mine)
            def _():
                pltpu.make_async_copy(src, dst, col_recv.at[clus]).start()

            @pl.when(jnp.logical_not(mine))
            def _():
                remote(
                    src, dst, col_send.at[2 * j + part], col_recv.at[clus], (head, fsdp, part)
                ).start()

    own_rows = pltpu.make_async_copy(
        feats.at[pl.ds(pl.multiple_of(core * BLK, BLK), BLK)], rows.at[clus], local_sem
    )
    own_rows.start()
    send(4, 5)

    @pl.loop(0, NC)
    def _(i):
        remote(
            wb.at[0, :, pl.ds(0, HD)],
            wall.at[core, i, fsdp],
            col_send.at[0],
            col_recv.at[i],
            (clus, fsdp, 1 - core),
        ).wait_recv()

    def z_copy(i):
        other = (fsdp + i) % NZ
        return remote(
            wall.at[core, :, fsdp],
            wall.at[core, :, fsdp],
            z_send.at[i],
            z_recv.at[i],
            (clus, other, core),
        )

    @pl.loop(1, NZ)
    def _(i):
        z_copy(i).start()

    def cot_copy(j, block):
        head = core * PER + j
        src = grad_out.at[
            pl.ds(block * BLK, BLK), pl.ds(pl.multiple_of(j * HD, HD), HD)
        ]
        return head, src, cot_out.at[clus]

    arrived(0, 1)
    send(2, 3, 8, 9, 12, 13)

    @pl.loop(0, PER)
    def _(i):
        j = (i + clus) % PER
        for block in (0, 1):
            head, src, dst = cot_copy(j, block)
            mine = jnp.logical_and(head == clus, core == block)

            @pl.when(mine)
            def _():
                pltpu.make_async_copy(src, dst, cot_recv.at[clus]).start()

            @pl.when(jnp.logical_not(mine))
            def _():
                remote(
                    src, dst, cot_send.at[2 * j + block], cot_recv.at[clus], (head, fsdp, block)
                ).start()


    @pl.loop(1, NZ)
    def _(i):
        other = (fsdp + NZ - i) % NZ
        remote(
            wall.at[core, :, other],
            wall.at[core, :, other],
            z_send.at[i],
            z_recv.at[i],
            (clus, other, core),
        ).wait_recv()

    swap = remote(
        wall.at[core], wall.at[core], swap_send, swap_recv, (clus, fsdp, 1 - core)
    )
    swap.start()
    arrived(4, 5)
    send(6, 7)
    arrived(2, 3)
    send(16, 17)
    remote(
        wall.at[1 - core], wall.at[1 - core], swap_send, swap_recv, (clus, fsdp, 1 - core)
    ).wait_recv()
    own_rows.wait()

    shared = []

    def project(dx, dy):
        src = at(dx, dy)
        index = len(shared)
        weights = jnp.concatenate(
            [wall[0].reshape(D, HD), wall[1].reshape(D, HD)], axis=1
        )
        both = lax.dot_general(rows[src], weights, NN, preferred_element_type=F32)
        q_out[src] = both[:, :HD].astype(BF)
        keys = both[:, HD:]
        mine = 2 * src + core
        kv_out[mine, 0] = keys.astype(BF)
        kv_out[mine, 1] = keys.T.astype(BF)
        share = remote(
            kv_out.at[mine],
            kv_out.at[mine],
            kv_send.at[index],
            kv_recv.at[index],
            (clus, fsdp, 1 - core),
        )
        share.start()
        theirs = 2 * src + 1 - core
        shared.append(
            (
                share,
                remote(
                    kv_out.at[theirs],
                    kv_out.at[theirs],
                    kv_send.at[index],
                    kv_recv.at[index],
                    (clus, fsdp, 1 - core),
                ),
            )
        )

    project(0, 0)
    arrived(8, 9, 12, 13)
    send(10, 11, 14, 15)
    project(1, 0)
    project(-1, 0)
    project(0, 1)
    arrived(16, 17)
    send(18, 19)
    project(0, -1)
    project(1, 1)
    project(-1, 1)
    project(1, -1)
    project(-1, -1)
    arrived(6, 7)
    project(2, 0)
    project(0, 2)
    arrived(10, 11, 14, 15)
    project(2, 1)
    project(2, -1)
    project(1, 2)
    project(-1, 2)
    arrived(18, 19)
    project(2, 2)

    @pl.loop(0, NC)
    def _(i):
        remote(
            grad_out.at[pl.ds(0, BLK), pl.ds(0, HD)],
            cot_out.at[i],
            cot_send.at[0],
            cot_recv.at[i],
            (clus, fsdp, 1 - core),
        ).wait_recv()

    @pl.loop(0, PER)
    def _(j):
        for part in (0, 1):
            head, src, dst = column_copy(j, part)
            _, csrc, cdst = cot_copy(j, part)

            @pl.when(jnp.logical_not(jnp.logical_and(head == clus, core == part)))
            def _():
                remote(
                    src, dst, col_send.at[2 * j + part], col_recv.at[clus], (head, fsdp, part)
                ).wait_send()
                remote(
                    csrc, cdst, cot_send.at[2 * j + part], cot_recv.at[clus], (head, fsdp, part)
                ).wait_send()

    @pl.loop(1, NZ)
    def _(i):
        z_copy(i).wait_send()

    swap.wait_send()
    for label in range(20):
        for half in (0, 1):
            src, _, part = plan[half, label]
            ring(half, label, src, part, label in (0, 1, 4, 5)).wait_send()
    for share, theirs in shared:
        share.wait_send()
        theirs.wait_recv()


def attend_kernel(q, kv, cot, col_block, col_count, out, dqt, total):
    clus, fsdp, core = here()
    total[...] = jnp.zeros_like(total)

    def stage_one(i):
        block = 2 * NZ * i + 2 * fsdp + core
        cols = [col_block[k, block] for k in range(NCOL)]
        cols = [(c // (2 * NZ)) * 2 + c % 2 for c in cols]
        live = col_count[block] == NCOL
        query, grad = q[i], cot[i]
        pair = jnp.concatenate([query, grad], axis=0)
        both = [
            lax.dot_general(kv[c, 0], pair, NT, preferred_element_type=F32) for c in cols
        ]
        return cols, live, query, grad, both

    def stage_two(cols, live, query, grad, both):
        scores = [x[:, :BLK] for x in both]
        scores[-1] = jnp.where(live, scores[-1], -1e30)
        top = functools.reduce(jnp.maximum, scores)
        top = jnp.max(top, axis=0, keepdims=True)
        expos = [jnp.exp2((x - top) * LOG2) for x in scores]
        norm = jnp.sum(functools.reduce(jnp.add, expos), axis=0, keepdims=True)
        inv = 1.0 / norm
        probs = [x * inv for x in expos]
        delta = functools.reduce(jnp.add, [p * x[:, BLK:] for p, x in zip(probs, both)])
        delta = jnp.sum(delta, axis=0, keepdims=True)
        ds = [(p * SCALE * (x[:, BLK:] - delta)).astype(BF) for p, x in zip(probs, both)]
        return ds, [p.astype(BF) for p in probs]

    def stage_three(i, cols, query, grad, ds, pb):
        keys_t = jnp.concatenate([kv[c, 1] for c in cols], axis=1)
        right = jnp.concatenate(
            [jnp.concatenate(ds, axis=0), jnp.concatenate(pb, axis=0)], axis=1
        )
        both_t = lax.dot_general(keys_t, right, NN, preferred_element_type=F32)
        dqt[:, pl.ds(pl.multiple_of(i * BLK, BLK), BLK)] = both_t[:, :BLK].astype(BF)
        out[i] = both_t[:, BLK:].T.astype(BF)
        pair = jnp.concatenate([query, grad], axis=0)
        for k, c in enumerate(cols):
            total[c // 2, c % 2] += lax.dot_general(
                jnp.concatenate([ds[k], pb[k]], axis=1), pair, NN, preferred_element_type=F32
            )

    GROUP = 8

    def step(n, carry):
        items = [n * GROUP + g for g in range(GROUP)]
        ones = [stage_one(i) for i in items]
        twos = [stage_two(*o) for o in ones]
        for i, o, t in zip(items, ones, twos):
            stage_three(i, o[0], o[2], o[3], *t)
        return carry

    lax.fori_loop(0, NC // GROUP, step, 0)


def scatter_kernel(
    feats,
    out_blocks,
    dqt,
    dkv,
    out,
    grad_q,
    grad_k,
    other,
    dkt,
    part_send,
    part_recv,
    part_own,
    z_out,
    z_in,
    fin,
    dk_sem,
    out_send,
    out_recv,
    half_send,
    half_recv,
    z_send,
    z_recv,
    fin_send,
    fin_recv,
):
    clus, fsdp, core = here()
    greet(clus, fsdp, core)
    sibling = (clus, fsdp, 1 - core)
    give = remote(dkv.at[:, 1 - core], other, dk_sem.at[0], dk_sem.at[1], sibling)

    def out_spot():
        return out.at[
            pl.ds(pl.multiple_of(core * BLK, BLK), BLK),
            pl.ds(pl.multiple_of((clus % PER) * HD, HD), HD),
        ]

    def out_copy(s):
        return remote(
            out_blocks.at[s],
            out_spot(),
            out_send.at[s],
            out_recv.at[2 * (clus % PER) + core],
            (s, fsdp, clus // PER),
        )

    own_out = core == clus // PER

    def send_out():
        @pl.loop(0, NC)
        def _(i):
            s = (i + clus) % NC
            mine = jnp.logical_and(s == clus, own_out)

            @pl.when(mine)
            def _():
                pltpu.make_async_copy(
                    out_blocks.at[s], out_spot(), out_recv.at[2 * (clus % PER) + core]
                ).start()

            @pl.when(jnp.logical_not(mine))
            def _():
                out_copy(s).start()

    def half_copy(t):
        return remote(
            part_send.at[t], part_recv.at[t], half_send.at[t], half_recv.at[t], sibling
        )

    HOPS = ((-2, -4), (-1, -3), (1, 3), (-1, -1), (1, 1), (-2, -2), (2, 2))

    def turn(t, steps):
        return (fsdp + NZ + (steps if t == 0 else -steps)) % NZ

    def z_copy(t, i):
        hops, owner = HOPS[i]
        return remote(
            z_out.at[t, turn(t, owner)],
            z_in.at[t, i],
            z_send.at[t, i],
            z_recv.at[t, i],
            (clus, turn(t, hops), core),
        )

    def stage_one(t):
        for i in range(5):
            z_copy(t, i).start()

    def stage_two(t):
        for i in range(3):
            z_copy(t, i).wait_recv()
        down, up = turn(t, -2), turn(t, 2)
        for k in range(PER):
            total = part_own[t, k, down] + z_in[t, 0, k].astype(F32) + z_in[t, 1, k].astype(F32)
            z_out[t, down, k] = total.astype(BF)
        z_copy(t, 5).start()
        for k in range(PER):
            z_out[t, up, k] = (part_own[t, k, up] + z_in[t, 2, k].astype(F32)).astype(BF)
        z_copy(t, 6).start()

    CH = 2 * BLK

    def chunk(lhs, n, side):
        cols = pl.ds(pl.multiple_of(side * HALF + n * CH, CH), CH)
        part = lax.dot_general(
            lhs[...],
            feats[:, :, cols].reshape(NC * BLK, CH),
            NN,
            preferred_element_type=F32,
        )
        return [part[:, k * BLK : (k + 1) * BLK].T.reshape(NZ, WROWS, HD) for k in (0, 1)]

    def for_sibling(t, lhs):
        for n in range(PER // 2):
            for k, piece in enumerate(chunk(lhs, n, 1 - core)):
                part_send[t, 2 * n + k] = piece.astype(BF)

    def for_self(t, lhs):
        for n in range(PER // 2):
            for k, piece in enumerate(chunk(lhs, n, core)):
                part_own[t, 2 * n + k] = piece

    def add_sibling(t):
        half_copy(t).wait_recv()
        for k in range(PER):
            total = part_own[t, k] + part_recv[t, k].astype(F32)
            part_own[t, k] = total
            z_out[t, :, k] = total.astype(BF)
        stage_one(t)

    for_sibling(0, dqt)
    for_self(0, dqt)
    greeted()
    half_copy(0).start()
    give.start()
    send_out()
    add_sibling(0)
    give.wait_recv()
    for s in range(NC):
        total = (dkv[s, core] + other[s]).astype(BF).astype(F32)
        dkt[:, s * BLK : (s + 1) * BLK] = total.T.astype(BF)
    for_sibling(1, dkt)
    half_copy(1).start()
    for_self(1, dkt)
    add_sibling(1)
    stage_two(0)
    stage_two(1)

    def fin_copy(t, k):
        dest = (grad_q, grad_k)[t]
        to = core * PER + k
        return (
            to,
            fin.at[t, k],
            dest.at[:, pl.ds(pl.multiple_of((clus % PER) * HD, HD), HD)],
            fin_recv.at[t, clus % PER],
        )

    def finish(t):
        for i in range(3, 7):
            z_copy(t, i).wait_recv()
        for k in range(PER):
            total = part_own[t, k, fsdp]
            for i in range(3, 7):
                total += z_in[t, i, k].astype(F32)
            fin[t, k] = total

        @pl.loop(0, PER)
        def _(i):
            k = (i + clus) % PER
            to, src, dst, recv = fin_copy(t, k)

            @pl.when(to == clus)
            def _():
                pltpu.make_async_copy(src, dst, recv).start()

            @pl.when(to != clus)
            def _():
                remote(src, dst, fin_send.at[t, k], recv, (to, fsdp, clus // PER)).start()

    finish(0)

    give.wait_send()
    for t in (0, 1):
        half_copy(t).wait_send()
        for i in range(5):
            z_copy(t, i).wait_send()

    @pl.loop(0, NC)
    def _(s):
        @pl.when(jnp.logical_not(jnp.logical_and(s == clus, own_out)))
        def _():
            out_copy(s).wait_send()

    for m in range(PER):
        for block in (0, 1):
            remote(
                out_blocks.at[0],
                out.at[pl.ds(block * BLK, BLK), pl.ds(m * HD, HD)],
                out_send.at[0],
                out_recv.at[2 * m + block],
                sibling,
            ).wait_recv()

    finish(1)

    for t in (0, 1):
        for i in (5, 6):
            z_copy(t, i).wait_send()

        @pl.loop(0, PER)
        def _(k):
            to, src, dst, recv = fin_copy(t, k)

            @pl.when(to != clus)
            def _():
                remote(src, dst, fin_send.at[t, k], recv, (to, fsdp, clus // PER)).wait_send()

    for m in range(PER):
        for t in (0, 1):
            remote(
                fin.at[t, 0],
                (grad_q, grad_k)[t].at[:, pl.ds(m * HD, HD)],
                fin_send.at[t, 0],
                fin_recv.at[t, m],
                sibling,
            ).wait_recv()


def place_kernel(*refs):
    copies = [
        pltpu.make_async_copy(refs[i], refs[3 + i], refs[6].at[i]) for i in range(3)
    ]
    for copy in copies:
        copy.start()
    for copy in copies:
        copy.wait()


HB = pl.BlockSpec(memory_space=pltpu.HBM)
VM = pl.BlockSpec(memory_space=pltpu.VMEM)
SM = pl.BlockSpec(memory_space=pltpu.SMEM)
DMA = pltpu.SemaphoreType.DMA
MIB = 1 << 20


def shape(dims, kind):
    return jax.ShapeDtypeStruct(dims, kind)


def on_device(feats, w_query, w_keyval, grad_out, col_block, col_count):
    feats_all, query, keyval, cots = pl.pallas_call(
        gather_kernel,
        name="gather_project",
        out_shape=(
            shape((NC, BLK, D), BF),
            shape((NC, BLK, HD), BF),
            shape((2 * NC, 2, BLK, HD), BF),
            shape((NC, BLK, HD), BF),
        ),
        in_specs=[HB, HB, HB, HB],
        out_specs=(VM, VM, VM, VM),
        scratch_shapes=[
            pltpu.VMEM((2, WROWS, HALF), F32),
            pltpu.VMEM((2, WROWS, HALF), BF),
            pltpu.VMEM((2, NC, NZ, WROWS, HD), BF),
            DMA((2,)),
            DMA((40,)),
            DMA((40,)),
            DMA,
            DMA((16,)),
            DMA((NC,)),
            DMA((NZ,)),
            DMA((NZ,)),
            DMA,
            DMA,
            DMA((16,)),
            DMA((NC,)),
            DMA((NC,)),
            DMA((NC,)),
        ],
        compiler_params=pltpu.CompilerParams(
            collective_id=1, has_side_effects=True, vmem_limit_bytes=24 * MIB
        ),
        cost_estimate=pl.CostEstimate(
            flops=2 * D * D * 256, bytes_accessed=18 << 20, transcendentals=0
        ),
    )(*(pltpu.with_memory_space_constraint(x, pltpu.HBM) for x in (feats, w_query, w_keyval, grad_out)))
    out_blocks, dqt, dkv = pl.pallas_call(
        attend_kernel,
        name="attend",
        out_shape=(
            shape((NC, BLK, HD), BF),
            shape((HD, NC * BLK), BF),
            shape((NC, 2, BLK, HD), F32),
        ),
        in_specs=[VM, VM, VM, SM, SM],
        out_specs=(VM, VM, VM),
        compiler_params=pltpu.CompilerParams(vmem_limit_bytes=16 * MIB),
        cost_estimate=pl.CostEstimate(
            flops=12 * NC * BLK * 640 * HD, bytes_accessed=6 * MIB, transcendentals=NC * BLK * 640
        ),
    )(query, keyval, cots, col_block.T, col_count)
    results = pl.pallas_call(
        scatter_kernel,
        name="scatter_grads",
        out_shape=(
            shape((2 * BLK, HALF), BF),
            shape((WROWS, HALF), F32),
            shape((WROWS, HALF), F32),
        ),
        in_specs=[VM, VM, VM, VM],
        out_specs=(VM, VM, VM),
        scratch_shapes=[
            pltpu.VMEM((NC, BLK, HD), F32),
            pltpu.VMEM((HD, NC * BLK), BF),
            pltpu.VMEM((2, PER, NZ, WROWS, HD), BF),
            pltpu.VMEM((2, PER, NZ, WROWS, HD), BF),
            pltpu.VMEM((2, PER, NZ, WROWS, HD), F32),
            pltpu.VMEM((2, NZ, PER, WROWS, HD), BF),
            pltpu.VMEM((2, 7, PER, WROWS, HD), BF),
            pltpu.VMEM((2, PER, WROWS, HD), F32),
            DMA((2,)),
            DMA((NC,)),
            DMA((NC,)),
            DMA((2,)),
            DMA((2,)),
            DMA((2, 7)),
            DMA((2, 7)),
            DMA((2, PER)),
            DMA((2, PER)),
        ],
        compiler_params=pltpu.CompilerParams(
            collective_id=2, has_side_effects=True, vmem_limit_bytes=24 * MIB
        ),
        cost_estimate=pl.CostEstimate(
            flops=2 * D * D * 256, bytes_accessed=12 * MIB, transcendentals=0
        ),
    )(feats_all, out_blocks, dqt, dkv)
    return pl.pallas_call(
        place_kernel,
        name="place",
        out_shape=tuple(pltpu.HBM(r.shape, r.dtype) for r in results),
        in_specs=[VM] * 3,
        out_specs=(HB,) * 3,
        scratch_shapes=[DMA((3,))],
        compiler_params=pltpu.CompilerParams(vmem_limit_bytes=16 * MIB),
    )(*results)


def solution(mesh):
    return jax.shard_map(
        on_device,
        mesh=mesh,
        in_specs=(
            P(("clus", "fsdp"), None),
            P(("clus", "fsdp"), "head"),
            P(("clus", "fsdp"), "head"),
            P(("clus", "fsdp"), "head"),
            P(),
            P(),
        ),
        out_specs=(
            P(("clus", "fsdp"), "head"),
            P(("clus", "fsdp"), "head"),
            P(("clus", "fsdp"), "head"),
        ),
        check_vma=False,
    )
```
